768 devices in a mesh: dp: 24 (over y_lo, z), tensor: 32 (over x, y_hi, core).
Axes of the slice: x: 4, y: 8 (y_hi: 4, y_lo: 2; y = y_hi * 2 + y_lo), z: 12, core: 2. Of those that a mesh axis runs over, the one named last changes fastest.
Arguments:
- expert_rows: bfloat16 [24, 32, 1056, 768], P('dp', 'tensor'), may hold values from -0.109375 to 0.109375
- expert_ids: int32 [98304, 2], P(('dp', 'tensor')), may hold values from 0 to 7, all different within a row; in each aligned block of 128 rows (0 to 127, 128 to 255, ...) at most 33 rows name the same one
- gate_logits: float32 [98304, 2], P(('dp', 'tensor')), may hold values from -6 to 6
- layer_input: bfloat16 [98304, 3072], P(('dp', 'tensor')), may hold values from -24 to 24
- out_grad: bfloat16 [98304, 3072], P(('dp', 'tensor')), may hold values from -6 to 6
Outputs:
- slot_grad: bfloat16 [24, 32, 1056, 768], P('dp', 'tensor')
- logit_grad: float32 [98304, 2], P(('dp', 'tensor'))
- router_grad: float32 [3072, 8], P(('dp', 'tensor'))
The draws below stay inside these ranges and needn't reach their ends.
Inputs may be any that keep to these rules, and one draw needn't show every extreme that they name: `expert_ids`: the two experts of a token differ. Among the 128 rows of one device no expert is named by more than 33 rows, and in some devices one expert is named by exactly 33 rows.
All inputs are finite; a program needn't handle non-finite values.
Results may differ from the reference program's by a relative error of at most 0.0029.
Values may be sent and summed in bfloat16 or wider, within the bound.
A program may use at most 64 MiB of HBM per device.

```python
import math
import jax
import jax.numpy as jnp
import numpy as np
from jax import lax

D = 3072
EXPERTS = 8
TOK_DEV = 128
C_DEV = 33
ET = 4
DK = 768
CAP = 1056
TOKENS = 98304
N_DP = 24
N_TENSOR = 32


def spiked(values, own_key, source, target, blocks, factor):
    owner, partner = [(jnp.arange(values.shape[axis_at]) // (values.shape[axis_at] // blocks)).reshape([-1 if axis == axis_at else 1 for axis in range(values.ndim)]) for axis_at in (source, target)]
    chosen = jax.random.permutation(own_key, blocks)[partner]
    strong = (owner == chosen) | (owner == (partner + blocks // 2) % blocks)
    return jnp.where(strong, factor * values, values)


def level_of(stream_key, dims, shards, low, high):
    level = 1.0
    for position, shards_of in shards:
        steps = jax.random.uniform(jax.random.fold_in(jax.random.fold_in(stream_key, 6), position), (shards_of,), jnp.float32, low / len(shards), high / len(shards))
        level = level * jnp.repeat(jnp.exp(steps), dims[position] // shards_of).reshape((-1,) + (1,) * (len(dims) - 1 - position))
    return level


def routed_block(key, own, number, rows, number_of, top, most, skew):
    order = jax.random.permutation(key, number_of)
    crowded, ordinary = shares(number_of, rows * top, most, skew, True), shares(number_of, rows * top, most, skew, False)
    places = jnp.arange(number_of)

    def named(tallies, offset_by):
        used = int((tallies > 0).sum())
        fixed = max(1, used // 4)
        passed = fixed + (places - fixed + offset_by * (used - fixed)) % max(1, number_of - fixed)
        return jnp.zeros((number_of,), jnp.int32).at[order[jnp.where(places < fixed, places, passed)]].set(jnp.asarray(tallies, jnp.int32))

    tallies = jnp.where(number % 4 == 0, named(crowded, number // 4), named(ordinary, number - number // 4 - 1))
    mixed = jax.random.permutation(jax.random.fold_in(own, 3), number_of)
    source_of, sink = mixed[0:number_of // 2 * 2:2], mixed[1:number_of // 2 * 2:2]
    margin = jnp.minimum(tallies[source_of] - 1, most - tallies[sink]) // 2
    margin = jnp.where((source_of == order[0]) | (sink == order[0]) | (tallies[sink] == 0), 0, jnp.maximum(margin, 0))
    passed = jax.random.randint(jax.random.fold_in(own, 4), (number_of // 2,), 0, 1 << 20) % (margin + 1)
    tallies = tallies.at[source_of].add(-passed).at[sink].add(passed)
    items = jnp.searchsorted(jnp.cumsum(tallies), jnp.arange(rows * top), side="right").astype(jnp.int32)
    grid = items.reshape(top, rows).T
    grid = grid[jax.random.permutation(jax.random.fold_in(own, 1), rows)]
    offset_by = jax.random.randint(jax.random.fold_in(own, 2), (rows, 1), 0, top)
    return jnp.take_along_axis(grid, (jnp.arange(top)[None, :] + offset_by) % top, axis=1)


def shares(number_of, total, limit, slope, full):
    loads = [(1 << 20) // math.isqrt(standing ** slope) + 1 for standing in range(1, number_of + 1)]
    largest = limit if full else min(limit, max(-(-total // number_of), total * loads[0] // sum(loads)))
    least = 1 if total - largest >= number_of - 1 else 0
    holding, rest = [largest] + [least] * (number_of - 1), total - largest - least * (number_of - 1)
    while rest > 0:
        candidates = [i for i in range(1, number_of) if holding[i] < largest] or [i for i in range(1, number_of) if holding[i] < limit]
        whole, remaining = sum([loads[i] for i in candidates]), rest
        for i in candidates:
            extra = min(limit - holding[i], max(1, remaining * loads[i] // whole), rest)
            holding[i] = holding[i] + extra
            rest = rest - extra
    return np.array(holding)


def scatter_about(own_key, dims, width, most, shards=(), kind=jnp.bfloat16):
    array = jax.random.normal(own_key, dims, jnp.float32) * width
    if len(shards) > 0:
        array = level_of(own_key, dims, shards, -0.22, 0.18) * array
    return jnp.clip(array, min=-most, max=most).astype(kind)


def noise_with(stream_key, dims, width, limit, split, heavy, kind=jnp.bfloat16):
    values = width * jax.random.normal(stream_key, dims, jnp.float32)
    if split:
        values = values * level_of(stream_key, dims, split, -0.22, 0.18)
    return jnp.clip(spiked(values, jax.random.fold_in(stream_key, 3), *heavy), -limit, limit).astype(kind)


def setup_inputs(seed: int = 0) -> dict:
    seeds = jax.random.split(jax.random.key(seed), 6)
    expert_rows = scatter_about(seeds[0], (N_DP, EXPERTS * ET, CAP, DK), D ** -0.5, 0.109375, ((0, 24), (1, 32)))
    expert_ids_keys = jax.random.split(jax.random.fold_in(seeds[1], 1), TOKENS // TOK_DEV)
    expert_ids_turns = jax.random.permutation(jax.random.fold_in(seeds[1], 3), TOKENS // TOK_DEV)
    expert_ids = jax.vmap(lambda own, number: routed_block(jax.random.fold_in(seeds[1], 2), own, number, TOK_DEV, EXPERTS, 2, C_DEV, 2))(expert_ids_keys, expert_ids_turns).reshape((TOKENS, 2))
    gate_logits = scatter_about(seeds[2], (TOKENS, 2), 1.5, 6.0, ((0, 768),), jnp.float32)
    layer_input = noise_with(seeds[3], (TOKENS, D), 1.0, 24.0, ((0, 768),), (0, 1, 768, 6.0))
    out_grad = scatter_about(seeds[4], (TOKENS, D), 1.0, 6.0, ((0, 768),))
    return dict(expert_rows=expert_rows, expert_ids=expert_ids, gate_logits=gate_logits, layer_input=layer_input, out_grad=out_grad)


def group_block(pack):
    rows_g, ids_g, logits_g, grad_g = pack
    catalog = jnp.arange(EXPERTS, dtype=jnp.int32)
    chosen = (ids_g[:, :, None] == catalog[None, None, :]).astype(jnp.int32)
    hit_counts = jnp.sum(chosen, axis=1).reshape(N_TENSOR, TOK_DEV, EXPERTS)
    before = (jnp.cumsum(hit_counts, axis=1) - hit_counts).reshape(N_TENSOR * TOK_DEV, EXPERTS)
    slot_rank = jnp.take_along_axis(before, ids_g, axis=1).astype(jnp.int32)
    member = (jnp.arange(N_TENSOR * TOK_DEV, dtype=jnp.int32) // TOK_DEV).astype(jnp.int32)
    slot_of = (member[:, None] * C_DEV + slot_rank).astype(jnp.int32)
    col_parts = jnp.arange(ET, dtype=jnp.int32)
    column_rows = (ids_g[:, :, None] * ET + col_parts[None, None, :]).astype(jnp.int32)
    fetched = rows_g[column_rows, slot_of[:, :, None]].reshape(N_TENSOR * TOK_DEV, 2, D)
    grad32 = grad_g.astype(jnp.float32)
    scores = jnp.sum(fetched.astype(jnp.float32) * grad32[:, None, :], axis=2)
    first_prob = 1.0 / (1.0 + jnp.exp(logits_g[:, 1] - logits_g[:, 0]))
    second_prob = 1.0 / (1.0 + jnp.exp(logits_g[:, 0] - logits_g[:, 1]))
    weights = jnp.stack([first_prob, second_prob], axis=1)
    average = jnp.sum(weights * scores, axis=1, keepdims=True)
    logit_grad = weights * (scores - average)
    combined = jnp.sum(chosen.astype(jnp.float32) * logit_grad[:, :, None], axis=1).astype(jnp.bfloat16)
    scaled = (weights[:, :, None] * grad32[:, None, :]).astype(jnp.bfloat16)
    slot_grad = jnp.zeros(rows_g.shape, jnp.bfloat16).at[column_rows, slot_of[:, :, None]].set(scaled.reshape(N_TENSOR * TOK_DEV, 2, ET, DK))
    return slot_grad, logit_grad, combined


def reference(expert_rows, expert_ids, gate_logits, layer_input, out_grad):
    group_tokens = TOK_DEV * N_TENSOR
    slot_grad, logit_grad, combined = lax.map(group_block, (expert_rows, expert_ids.reshape(N_DP, group_tokens, 2), gate_logits.reshape(N_DP, group_tokens, 2), out_grad.reshape(N_DP, group_tokens, D)))
    combined = combined.reshape(TOKENS, EXPERTS)
    router_grad = jnp.dot(layer_input.T, combined, preferred_element_type=jnp.float32) * (TOKENS ** -0.5)
    return slot_grad, logit_grad.reshape(TOKENS, 2), router_grad
```

```python
import functools

import jax
import jax.numpy as jnp
from jax import lax
from jax.experimental import pallas as pl
from jax.experimental.pallas import tpu as pltpu
from jax.sharding import PartitionSpec as P

EXPERTS = 8
LANES = 128
F32 = jnp.float32
BF16 = jnp.bfloat16
MESH = pl.DeviceIdType.MESH


def iota(shape, axis):
    return lax.broadcasted_iota(jnp.int32, shape, axis)


def split3(x):
    hi = x.astype(BF16).astype(F32)
    mid = (x - hi).astype(BF16).astype(F32)
    return hi, mid, x - hi - mid


def kernel(
    n_dp,
    n_tensor,
    scale,
    rows_hbm,
    ids_ref,
    logits_ref,
    input_hbm,
    grad_hbm,
    slot_out,
    logit_out,
    router_out,
    rows,
    inputs,
    grads,
    send,
    recv,
    rows32,
    slot32,
    score_send,
    score_recv,
    term_send,
    term_recv,
    turned,
    part_send,
    part_recv,
    load_sem,
    send_sem,
    recv_sem,
    ssend_sem,
    srecv_sem,
    tsend_sem,
    trecv_sem,
    psend_sem,
    precv_sem,
):
    me = lax.axis_index("tensor")
    group = lax.axis_index("dp")
    members = n_tensor // EXPERTS
    capacity = rows.shape[0] // n_tensor
    full = capacity - 1
    segments = rows.shape[1] // LANES
    body = full * segments
    tokens = grads.shape[0]

    load_grads = pltpu.make_async_copy(grad_hbm, grads, load_sem.at[0])
    load_rows = pltpu.make_async_copy(rows_hbm, rows, load_sem.at[1])
    load_inputs = pltpu.make_async_copy(input_hbm, inputs, load_sem.at[2])
    load_grads.start()
    load_rows.start()
    load_inputs.start()

    barrier = pltpu.get_barrier_semaphore()

    @pl.loop(1, n_tensor)
    def _(i):
        peer = lax.rem(me + i, n_tensor)
        pl.semaphore_signal(barrier, inc=1, device_id={"tensor": peer}, device_id_type=MESH)

    @pl.loop(1, n_dp)
    def _(i):
        peer = lax.rem(group + i, n_dp)
        pl.semaphore_signal(barrier, inc=1, device_id={"dp": peer}, device_id_type=MESH)

    id0, id1 = ids_ref[0:1, :], ids_ref[1:2, :]
    logit0, logit1 = logits_ref[0:1, :], logits_ref[1:2, :]
    prob0 = 1.0 / (1.0 + jnp.exp(logit1 - logit0))
    prob1 = 1.0 / (1.0 + jnp.exp(logit0 - logit1))
    experts = iota((EXPERTS, tokens), 0)
    hot0 = jnp.where(experts == id0, 1.0, 0.0)
    hot1 = jnp.where(experts == id1, 1.0, 0.0)
    earlier = jnp.where(
        iota((tokens, tokens), 0) < iota((tokens, tokens), 1), 1.0, 0.0
    ).astype(BF16)
    before = jnp.dot((hot0 + hot1).astype(BF16), earlier, preferred_element_type=F32)
    rank0 = jnp.sum(hot0 * before, axis=0, keepdims=True).astype(jnp.int32)
    rank1 = jnp.sum(hot1 * before, axis=0, keepdims=True).astype(jnp.int32)
    slots = iota((LANES, tokens), 0)
    tail_row = iota((16, LANES), 0)

    load_grads.wait()
    pl.semaphore_wait(barrier, n_tensor - 1 + n_dp - 1)

    def remote_block(index, peer):
        return pltpu.make_async_remote_copy(
            src_ref=send.at[peer],
            dst_ref=recv.at[index],
            send_sem=send_sem.at[peer],
            recv_sem=recv_sem.at[index],
            device_id={"tensor": peer},
            device_id_type=MESH,
        )

    def pair(i):
        step = lax.rem(i // 2 + 1, 4)
        return step, lax.rem(i, 2)

    my_expert = me // members

    def expert_at(i, sign):
        step, other = pair(i)
        column = lax.rem(my_expert // 2 + sign * step + 4, 4)
        half = lax.rem(lax.rem(my_expert, 2) + other, 2)
        return column * 2 + half

    @pl.loop(0, EXPERTS)
    def _(i):
        expert = expert_at(i, 1)
        key0 = jnp.where(id0 == expert, rank0, -1)
        key1 = jnp.where(id1 == expert, rank1, -1)
        placing = jnp.where((slots == key0) | (slots == key1), 1.0, 0.0).astype(BF16)
        prob = jnp.where(id0 == expert, prob0, jnp.where(id1 == expert, prob1, 0.0))
        hi, mid, lo = split3(prob)
        parts = jnp.where(
            tail_row == segments,
            hi,
            jnp.where(tail_row == segments + 1, mid, jnp.where(tail_row == segments + 2, lo, 0.0)),
        ).astype(BF16)
        slot_probs = lax.dot_general(
            parts, placing, (((1,), (1,)), ((), ())), preferred_element_type=F32
        )
        for k in range(members):
            peer = expert * members + k
            packed = jnp.dot(
                placing[: full + 16],
                grads[:, k * segments * LANES : (k + 1) * segments * LANES],
                preferred_element_type=F32,
            )
            tail = slot_probs
            for j in range(segments):
                piece = packed[:, j * LANES : (j + 1) * LANES]
                send[peer, j * full : (j + 1) * full, :] = piece[:full].astype(BF16)
                tail = jnp.where(tail_row == j, piece[full : full + 1], tail)
            send[peer, body : body + 16, :] = tail.astype(BF16)

            @pl.when(peer != me)
            def _():
                remote_block(me, peer).start()

            @pl.when(peer == me)
            def _():
                pltpu.make_async_copy(send.at[me], recv.at[me], recv_sem.at[me]).start()

    load_rows.wait()

    @pl.loop(0, rows.shape[0] // 32)
    def _(i):
        at = pl.multiple_of(i * 32, 32)
        for j in range(segments):
            rows32[j, pl.ds(at, 32), :] = rows[
                pl.ds(at, 32), j * LANES : (j + 1) * LANES
            ].astype(F32)

    diagonal = iota((full, LANES), 0) == iota((full, LANES), 1)
    lane = iota((1, LANES), 1)

    def remote_scores(index, peer):
        return pltpu.make_async_remote_copy(
            src_ref=score_send.at[peer],
            dst_ref=score_recv.at[index],
            send_sem=ssend_sem.at[peer],
            recv_sem=srecv_sem.at[index],
            device_id={"tensor": peer},
            device_id_type=MESH,
        )

    @pl.loop(0, n_tensor)
    def _(i):
        source = expert_at(i // members, -1) * members + lax.rem(i, members)
        pltpu.make_async_copy(send.at[source], recv.at[source], recv_sem.at[source]).wait()
        at = source * capacity
        tail = recv[source, body : body + 16, :].astype(F32)
        prob = (
            tail[segments : segments + 1]
            + tail[segments + 1 : segments + 2]
            + tail[segments + 2 : segments + 3]
        )
        prob_column = jnp.sum(jnp.where(diagonal, prob, 0.0), axis=1, keepdims=True)
        prob_last = jnp.sum(jnp.where(lane == full, prob, 0.0), axis=1, keepdims=True)
        products = jnp.zeros((full, LANES), F32)
        last = jnp.zeros((1, LANES), F32)
        for j in range(segments):
            piece = recv[source, j * full : (j + 1) * full, :].astype(F32)
            products += piece * rows32[j, pl.ds(at, full), :]
            slot32[j, pl.ds(at, full), :] = piece * prob_column
            row = tail[j : j + 1]
            last += row * rows32[j, pl.ds(at + full, 1), :]
            slot32[j, pl.ds(at + full, 1), :] = row * prob_last
        sums = jnp.sum(products, axis=1, keepdims=True)
        line = jnp.sum(jnp.where(diagonal, sums, 0.0), axis=0, keepdims=True)
        last_sum = jnp.sum(last, axis=1, keepdims=True)
        score_send[source] = jnp.where(lane == full, last_sum, line)

        @pl.when(source != me)
        def _():
            remote_scores(me, source).start()

        @pl.when(source == me)
        def _():
            pltpu.make_async_copy(
                score_send.at[me], score_recv.at[me], srecv_sem.at[me]
            ).start()

    ranks = iota((LANES, tokens), 0)
    chosen0 = jnp.where(ranks == rank0, 1.0, 0.0).astype(BF16)
    chosen1 = jnp.where(ranks == rank1, 1.0, 0.0).astype(BF16)
    load_inputs.wait()

    @pl.loop(0, n_tensor)
    def _(i):
        pltpu.make_async_copy(score_send.at[i], score_recv.at[i], srecv_sem.at[i]).wait()

    scores = jnp.zeros((EXPERTS, LANES), F32)
    for expert in range(EXPERTS):
        total = score_recv[expert * members]
        for k in range(1, members):
            total += score_recv[expert * members + k]
        scores = jnp.where(iota((EXPERTS, LANES), 0) == expert, total, scores)
    hi, mid, lo = split3(scores)
    terms = [part.astype(BF16) for part in (hi, mid, lo)]

    def looked_up(chosen, hot):
        found = jnp.zeros((EXPERTS, tokens), F32)
        for term in terms:
            found += jnp.dot(term, chosen, preferred_element_type=F32)
        return jnp.sum(found * hot, axis=0, keepdims=True)

    score0 = looked_up(chosen0, hot0)
    score1 = looked_up(chosen1, hot1)
    average = prob0 * score0 + prob1 * score1
    slope0 = prob0 * (score0 - average)
    slope1 = prob1 * (score1 - average)
    logit_out[0:1, :] = slope0
    logit_out[1:2, :] = slope1
    combined = (hot0 * slope0 + hot1 * slope1).astype(BF16)

    for g in range(n_dp):
        term_send[g] = jnp.dot(
            combined, inputs[:, g * LANES : (g + 1) * LANES], preferred_element_type=F32
        )

    def remote_term(index, peer):
        return pltpu.make_async_remote_copy(
            src_ref=term_send.at[peer],
            dst_ref=term_recv.at[index],
            send_sem=tsend_sem.at[peer],
            recv_sem=trecv_sem.at[index],
            device_id={"dp": peer},
            device_id_type=MESH,
        )

    @pl.loop(1, n_dp)
    def _(i):
        remote_term(group, lax.rem(group + i, n_dp)).start()

    own_term = pltpu.make_async_copy(
        term_send.at[group], term_recv.at[group], trecv_sem.at[group]
    )
    own_term.start()

    @pl.loop(0, rows.shape[0] // 32)
    def _(i):
        at = pl.multiple_of(i * 32, 32)
        for j in range(segments):
            slot_out[pl.ds(at, 32), j * LANES : (j + 1) * LANES] = slot32[
                j, pl.ds(at, 32), :
            ].astype(BF16)

    @pl.loop(0, n_dp)
    def _(i):
        pltpu.make_async_copy(term_send.at[i], term_recv.at[i], trecv_sem.at[i]).wait()

    total = term_recv[0]
    for g in range(1, n_dp):
        total += term_recv[g]

    square = jnp.concatenate([total, jnp.zeros((LANES - EXPERTS, LANES), F32)], axis=0)
    turned[...] = jnp.transpose(square)
    owned = LANES // n_tensor
    lines = turned[pl.ds(0, n_tensor, stride=owned), :]
    for j in range(1, owned):
        lines += pltpu.roll(turned[pl.ds(j, n_tensor, stride=owned), :], j * EXPERTS, 1)
    for i in range(n_tensor):
        part_send[i] = lines[i : i + 1]

    def remote_part(index, peer):
        return pltpu.make_async_remote_copy(
            src_ref=part_send.at[peer],
            dst_ref=part_recv.at[index],
            send_sem=psend_sem.at[peer],
            recv_sem=precv_sem.at[index],
            device_id={"tensor": peer},
            device_id_type=MESH,
        )

    @pl.loop(1, n_tensor)
    def _(i):
        remote_part(me, lax.rem(me + i, n_tensor)).start()

    own_part = pltpu.make_async_copy(part_send.at[me], part_recv.at[me], precv_sem.at[me])
    own_part.start()

    @pl.loop(1, n_tensor)
    def _(i):
        peer = lax.rem(me + i, n_tensor)
        remote_block(me, peer).wait_send()
        remote_scores(me, peer).wait_send()

    @pl.loop(1, n_dp)
    def _(i):
        remote_term(group, lax.rem(group + i, n_dp)).wait_send()

    @pl.loop(0, n_tensor)
    def _(i):
        pltpu.make_async_copy(part_send.at[i], part_recv.at[i], precv_sem.at[i]).wait()

    line = part_recv[0]
    for i in range(1, n_tensor):
        line += part_recv[i]
    line = line * scale
    for j in range(owned):
        router_out[j : j + 1, :] = line[:, j * EXPERTS : (j + 1) * EXPERTS]

    @pl.loop(1, n_tensor)
    def _(i):
        remote_part(me, lax.rem(me + i, n_tensor)).wait_send()


def on_device(expert_rows, expert_ids, gate_logits, layer_input, out_grad):
    n_tensor = lax.axis_size("tensor")
    n_dp = lax.axis_size("dp")
    slot_count, span = expert_rows.shape[2:]
    tokens, width = out_grad.shape
    capacity = slot_count // n_tensor
    segments = span // LANES
    block = (capacity - 1) * segments + 16
    owned = width // (n_dp * n_tensor)
    padded = slot_count + 8
    any_space = pl.BlockSpec(memory_space=pl.ANY)
    in_vmem = pl.BlockSpec(memory_space=pltpu.VMEM)
    dma = pltpu.SemaphoreType.DMA
    slot_grad, logit_grad, router_grad = pl.pallas_call(
        functools.partial(kernel, n_dp, n_tensor, (tokens * n_dp * n_tensor) ** -0.5),
        out_shape=(
            jax.ShapeDtypeStruct((slot_count, span), BF16),
            jax.ShapeDtypeStruct((2, tokens), F32),
            jax.ShapeDtypeStruct((owned, EXPERTS), F32),
        ),
        in_specs=[any_space, in_vmem, in_vmem, any_space, any_space],
        out_specs=(in_vmem, in_vmem, in_vmem),
        scratch_shapes=[
            pltpu.VMEM((slot_count, span), BF16),
            pltpu.VMEM((tokens, width), BF16),
            pltpu.VMEM((tokens, width), BF16),
            pltpu.VMEM((n_tensor, block, LANES), BF16),
            pltpu.VMEM((n_tensor, block, LANES), BF16),
            pltpu.VMEM((segments, padded, LANES), F32),
            pltpu.VMEM((segments, padded, LANES), F32),
            pltpu.VMEM((n_tensor, 1, LANES), F32),
            pltpu.VMEM((n_tensor, 1, LANES), F32),
            pltpu.VMEM((n_dp, EXPERTS, LANES), F32),
            pltpu.VMEM((n_dp, EXPERTS, LANES), F32),
            pltpu.VMEM((LANES, LANES), F32),
            pltpu.VMEM((n_tensor, 1, LANES), F32),
            pltpu.VMEM((n_tensor, 1, LANES), F32),
            dma((3,)),
            dma((n_tensor,)),
            dma((n_tensor,)),
            dma((n_tensor,)),
            dma((n_tensor,)),
            dma((n_dp,)),
            dma((n_dp,)),
            dma((n_tensor,)),
            dma((n_tensor,)),
        ],
        compiler_params=pltpu.CompilerParams(
            collective_id=0, has_side_effects=True, vmem_limit_bytes=56 * 2**20
        ),
    )(
        expert_rows.reshape(slot_count, span),
        expert_ids.T,
        gate_logits.T,
        layer_input,
        out_grad,
    )
    return slot_grad.reshape(expert_rows.shape), logit_grad.T, router_grad


def solution(mesh):
    in_specs = (
        P("dp", "tensor", None, None),
        P(("dp", "tensor"), None),
        P(("dp", "tensor"), None),
        P(("dp", "tensor"), None),
        P(("dp", "tensor"), None),
    )
    out_specs = (
        P("dp", "tensor", None, None),
        P(("dp", "tensor"), None),
        P(("dp", "tensor"), None),
    )
    return jax.shard_map(
        on_device, mesh=mesh, in_specs=in_specs, out_specs=out_specs, check_vma=False
    )
```

```python
import functools

import jax
import jax.numpy as jnp
from jax import lax
from jax.experimental import pallas as pl
from jax.experimental.pallas import tpu as pltpu
from jax.sharding import PartitionSpec as P

EXPERTS = 8
LANES = 128
F32 = jnp.float32
BF16 = jnp.bfloat16
MESH = pl.DeviceIdType.MESH


def iota(shape, axis):
    return lax.broadcasted_iota(jnp.int32, shape, axis)


def split3(x):
    hi = x.astype(BF16).astype(F32)
    mid = (x - hi).astype(BF16).astype(F32)
    return hi, mid, x - hi - mid


def wrapped(index, size):
    return jnp.where(index >= size, index - size, index)


def kernel(
    n_dp,
    n_tensor,
    scale,
    rows_hbm,
    ids_ref,
    logits_ref,
    input_hbm,
    grad_hbm,
    slot_out,
    logit_out,
    router_out,
    rows,
    inputs,
    grads,
    send,
    recv,
    rows32,
    slot32,
    score_send,
    score_recv,
    term_send,
    term_recv,
    turned,
    part_send,
    part_recv,
    load_sem,
    send_sem,
    recv_sem,
    ssend_sem,
    srecv_sem,
    tsend_sem,
    trecv_sem,
    psend_sem,
    precv_sem,
):
    me = lax.axis_index("tensor")
    group = lax.axis_index("dp")
    members = n_tensor // EXPERTS
    capacity = rows.shape[0] // n_tensor
    full = capacity - 1
    segments = rows.shape[1] // LANES
    body = full * segments
    tokens = grads.shape[0]

    barrier = pltpu.get_barrier_semaphore()

    def tensor_peer(i):
        return wrapped(me + i, n_tensor)

    def dp_peer(i):
        return wrapped(group + i, n_dp)

    @pl.loop(1, n_tensor, unroll=True)
    def _(i):
        pl.semaphore_signal(
            barrier, inc=1, device_id={"tensor": tensor_peer(i)}, device_id_type=MESH
        )

    @pl.loop(1, n_dp, unroll=True)
    def _(i):
        pl.semaphore_signal(barrier, inc=1, device_id={"dp": dp_peer(i)}, device_id_type=MESH)

    load_grads = pltpu.make_async_copy(grad_hbm, grads, load_sem.at[0])
    load_rows = pltpu.make_async_copy(rows_hbm, rows, load_sem.at[1])
    load_inputs = pltpu.make_async_copy(input_hbm, inputs, load_sem.at[2])
    load_grads.start()
    load_rows.start()
    load_inputs.start()

    id0, id1 = ids_ref[0:1, :], ids_ref[1:2, :]
    logit0, logit1 = logits_ref[0:1, :], logits_ref[1:2, :]
    prob0 = 1.0 / (1.0 + jnp.exp(logit1 - logit0))
    prob1 = 1.0 / (1.0 + jnp.exp(logit0 - logit1))
    experts = iota((EXPERTS, tokens), 0)
    hot0 = jnp.where(experts == id0, 1.0, 0.0)
    hot1 = jnp.where(experts == id1, 1.0, 0.0)
    earlier = jnp.where(
        iota((tokens, tokens), 0) < iota((tokens, tokens), 1), 1.0, 0.0
    ).astype(BF16)
    before = jnp.dot((hot0 + hot1).astype(BF16), earlier, preferred_element_type=F32)
    rank0 = jnp.sum(hot0 * before, axis=0, keepdims=True).astype(jnp.int32)
    rank1 = jnp.sum(hot1 * before, axis=0, keepdims=True).astype(jnp.int32)
    slots = iota((LANES, tokens), 0)
    tail_row = iota((16, LANES), 0)

    load_grads.wait()
    pl.semaphore_wait(barrier, n_tensor - 1 + n_dp - 1)

    def remote_block(index, peer):
        return pltpu.make_async_remote_copy(
            src_ref=send.at[peer],
            dst_ref=recv.at[index],
            send_sem=send_sem.at[peer],
            recv_sem=recv_sem.at[index],
            device_id={"tensor": peer},
            device_id_type=MESH,
        )

    column, row, core = me // 8, lax.rem(me // 2, 4), lax.rem(me, 2)

    def partner(i, sign):
        part, place = i // 8, i - 8
        middle = (part == 1) | (part == 2)
        along_y = jnp.where(middle, 1 + 2 * lax.rem(i, 2), jnp.where(part == 0, 2, 0))
        rest = jnp.where(middle, place // 2, lax.rem(i, 8))
        along_x = lax.rem(rest // 2 + 1, 4)
        return (
            lax.rem(column + sign * along_x + 4, 4) * 8
            + lax.rem(row + sign * along_y + 4, 4) * 2
            + lax.rem(core + rest + 1, 2)
        )

    def pack(expert):
        key0 = jnp.where(id0 == expert, rank0, -1)
        key1 = jnp.where(id1 == expert, rank1, -1)
        placing = jnp.where((slots == key0) | (slots == key1), 1.0, 0.0).astype(BF16)
        prob = jnp.where(id0 == expert, prob0, jnp.where(id1 == expert, prob1, 0.0))
        hi, mid, lo = split3(prob)
        parts = jnp.where(
            tail_row == segments,
            hi,
            jnp.where(tail_row == segments + 1, mid, jnp.where(tail_row == segments + 2, lo, 0.0)),
        ).astype(BF16)
        slot_probs = lax.dot_general(
            parts, placing, (((1,), (1,)), ((), ())), preferred_element_type=F32
        )
        for k in range(members):
            peer = expert * members + k
            packed = jnp.dot(
                placing[: full + 16],
                grads[:, k * segments * LANES : (k + 1) * segments * LANES],
                preferred_element_type=F32,
            )
            tail = slot_probs
            for j in range(segments):
                piece = packed[:, j * LANES : (j + 1) * LANES]
                send[peer, j * full : (j + 1) * full, :] = piece[:full].astype(BF16)
                tail = jnp.where(tail_row == j, piece[full : full + 1], tail)
            send[peer, body : body + 16, :] = tail.astype(BF16)

    half = row // 2

    @pl.loop(0, 4)
    def _(i):
        pack(lax.rem(column + i + 1, 4) * 2 + 1 - half)
        remote_block(me, partner(2 * i, 1)).start()
        remote_block(me, partner(2 * i + 1, 1)).start()

    @pl.loop(0, 4)
    def _(i):
        pack(lax.rem(column + i + 1, 4) * 2 + half)

    @pl.loop(8, n_tensor - 1)
    def _(i):
        remote_block(me, partner(i, 1)).start()

    pltpu.make_async_copy(send.at[me], recv.at[me], recv_sem.at[me]).start()

    load_rows.wait()

    @pl.loop(0, rows.shape[0] // 32)
    def _(i):
        at = pl.multiple_of(i * 32, 32)
        for j in range(segments):
            rows32[j, pl.ds(at, 32), :] = rows[
                pl.ds(at, 32), j * LANES : (j + 1) * LANES
            ].astype(F32)

    diagonal = iota((full, LANES), 0) == iota((full, LANES), 1)
    lane = iota((1, LANES), 1)

    def remote_scores(index, peer):
        return pltpu.make_async_remote_copy(
            src_ref=score_send.at[peer],
            dst_ref=score_recv.at[index],
            send_sem=ssend_sem,
            recv_sem=srecv_sem,
            device_id={"tensor": peer},
            device_id_type=MESH,
        )

    @pl.loop(0, n_tensor)
    def _(i):
        source = partner(i, -1)
        pltpu.make_async_copy(send.at[source], recv.at[source], recv_sem.at[source]).wait()
        at = source * capacity
        tail = recv[source, body : body + 16, :].astype(F32)
        prob = (
            tail[segments : segments + 1]
            + tail[segments + 1 : segments + 2]
            + tail[segments + 2 : segments + 3]
        )
        prob_column = jnp.sum(jnp.where(diagonal, prob, 0.0), axis=1, keepdims=True)
        prob_last = jnp.sum(jnp.where(lane == full, prob, 0.0), axis=1, keepdims=True)
        products = jnp.zeros((full, LANES), F32)
        last = jnp.zeros((1, LANES), F32)
        for j in range(segments):
            piece = recv[source, j * full : (j + 1) * full, :].astype(F32)
            products += piece * rows32[j, pl.ds(at, full), :]
            slot32[j, pl.ds(at, full), :] = piece * prob_column
            row = tail[j : j + 1]
            last += row * rows32[j, pl.ds(at + full, 1), :]
            slot32[j, pl.ds(at + full, 1), :] = row * prob_last
        sums = jnp.sum(products, axis=1, keepdims=True)
        line = jnp.sum(jnp.where(diagonal, sums, 0.0), axis=0, keepdims=True)
        last_sum = jnp.sum(last, axis=1, keepdims=True)
        score_send[source] = jnp.where(lane == full, last_sum, line)

        @pl.when(source != me)
        def _():
            remote_scores(me, source).start()

        @pl.when(source == me)
        def _():
            pltpu.make_async_copy(
                score_send.at[me], score_recv.at[me], srecv_sem
            ).start()

    ranks = iota((LANES, tokens), 0)
    chosen0 = jnp.where(ranks == rank0, 1.0, 0.0).astype(BF16)
    chosen1 = jnp.where(ranks == rank1, 1.0, 0.0).astype(BF16)
    load_inputs.wait()

    pltpu.make_async_copy(score_send, score_recv, srecv_sem).wait()
    scores = jnp.zeros((EXPERTS, LANES), F32)
    for expert in range(EXPERTS):
        total = score_recv[expert * members]
        for k in range(1, members):
            total += score_recv[expert * members + k]
        scores = jnp.where(iota((EXPERTS, LANES), 0) == expert, total, scores)
    hi, mid, lo = split3(scores)
    terms = [part.astype(BF16) for part in (hi, mid, lo)]

    def looked_up(chosen, hot):
        found = jnp.zeros((EXPERTS, tokens), F32)
        for term in terms:
            found += jnp.dot(term, chosen, preferred_element_type=F32)
        return jnp.sum(found * hot, axis=0, keepdims=True)

    score0 = looked_up(chosen0, hot0)
    score1 = looked_up(chosen1, hot1)
    average = prob0 * score0 + prob1 * score1
    slope0 = prob0 * (score0 - average)
    slope1 = prob1 * (score1 - average)
    logit_out[0:1, :] = slope0
    logit_out[1:2, :] = slope1
    combined = (hot0 * slope0 + hot1 * slope1).astype(BF16)

    def remote_term(index, peer):
        return pltpu.make_async_remote_copy(
            src_ref=term_send.at[peer],
            dst_ref=term_recv.at[index],
            send_sem=tsend_sem,
            recv_sem=trecv_sem,
            device_id={"dp": peer},
            device_id_type=MESH,
        )

    for k in range(members):
        term = jnp.dot(
            combined,
            inputs[:, k * segments * LANES : (k + 1) * segments * LANES],
            preferred_element_type=F32,
        )
        for j in range(segments):
            term_send[k * segments + j] = term[:, j * LANES : (j + 1) * LANES]

    @pl.loop(1, n_dp, unroll=True)
    def _(i):
        remote_term(group, dp_peer(i)).start()

    own_term = pltpu.make_async_copy(
        term_send.at[group], term_recv.at[group], trecv_sem
    )
    own_term.start()

    @pl.loop(0, rows.shape[0] // 32)
    def _(i):
        at = pl.multiple_of(i * 32, 32)
        for j in range(segments):
            slot_out[pl.ds(at, 32), j * LANES : (j + 1) * LANES] = slot32[
                j, pl.ds(at, 32), :
            ].astype(BF16)

    pltpu.make_async_copy(term_send, term_recv, trecv_sem).wait()
    total = term_recv[0]
    for g in range(1, n_dp):
        total += term_recv[g]

    square = jnp.concatenate([total, jnp.zeros((LANES - EXPERTS, LANES), F32)], axis=0)
    turned[...] = jnp.transpose(square)
    owned = LANES // n_tensor
    lines = turned[pl.ds(0, n_tensor, stride=owned), :]
    for j in range(1, owned):
        lines += pltpu.roll(turned[pl.ds(j, n_tensor, stride=owned), :], j * EXPERTS, 1)
    for i in range(n_tensor):
        part_send[i] = lines[i : i + 1]

    def remote_part(index, peer):
        return pltpu.make_async_remote_copy(
            src_ref=part_send.at[peer],
            dst_ref=part_recv.at[index],
            send_sem=psend_sem,
            recv_sem=precv_sem,
            device_id={"tensor": peer},
            device_id_type=MESH,
        )

    @pl.loop(1, n_tensor, unroll=True)
    def _(i):
        remote_part(me, tensor_peer(i)).start()

    own_part = pltpu.make_async_copy(part_send.at[me], part_recv.at[me], precv_sem)
    own_part.start()

    @pl.loop(1, n_tensor)
    def _(i):
        remote_block(me, tensor_peer(i)).wait_send()

    others = pl.ds(0, n_tensor - 1)
    pltpu.make_async_copy(score_send.at[others], score_recv.at[others], ssend_sem).wait()
    others_dp = pl.ds(0, n_dp - 1)
    pltpu.make_async_copy(term_send.at[others_dp], term_recv.at[others_dp], tsend_sem).wait()

    pltpu.make_async_copy(part_send, part_recv, precv_sem).wait()
    line = part_recv[0]
    for i in range(1, n_tensor):
        line += part_recv[i]
    line = line * scale
    for j in range(owned):
        router_out[j : j + 1, :] = line[:, j * EXPERTS : (j + 1) * EXPERTS]

    pltpu.make_async_copy(part_send.at[others], part_recv.at[others], psend_sem).wait()


def hand_over(chunks, slots, logits, router, slots_out, logits_out, router_out, sem):
    rows = slots.shape[0] // chunks
    parts = [pl.ds(i * rows, rows) for i in range(chunks)]
    copies = [
        pltpu.make_async_copy(slots.at[part], slots_out.at[part], sem.at[i])
        for i, part in enumerate(parts)
    ]
    copies.append(pltpu.make_async_copy(logits, logits_out, sem.at[chunks]))
    copies.append(pltpu.make_async_copy(router, router_out, sem.at[chunks + 1]))
    for copy in copies:
        copy.start()
    for copy in copies:
        copy.wait()


def on_device(expert_rows, expert_ids, gate_logits, layer_input, out_grad):
    n_tensor = lax.axis_size("tensor")
    n_dp = lax.axis_size("dp")
    slot_count, span = expert_rows.shape[2:]
    tokens, width = out_grad.shape
    capacity = slot_count // n_tensor
    segments = span // LANES
    block = (capacity - 1) * segments + 16
    owned = width // (n_dp * n_tensor)
    padded = slot_count + 8
    any_space = pl.BlockSpec(memory_space=pl.ANY)
    in_vmem = pl.BlockSpec(memory_space=pltpu.VMEM)
    dma = pltpu.SemaphoreType.DMA
    slot_grad, logit_grad, router_grad = pl.pallas_call(
        functools.partial(kernel, n_dp, n_tensor, (tokens * n_dp * n_tensor) ** -0.5),
        out_shape=(
            pltpu.VMEM((slot_count, span), BF16),
            pltpu.VMEM((2, tokens), F32),
            pltpu.VMEM((owned, EXPERTS), F32),
        ),
        in_specs=[any_space, in_vmem, in_vmem, any_space, any_space],
        out_specs=(in_vmem, in_vmem, in_vmem),
        scratch_shapes=[
            pltpu.VMEM((slot_count, span), BF16),
            pltpu.VMEM((tokens, width), BF16),
            pltpu.VMEM((tokens, width), BF16),
            pltpu.VMEM((n_tensor, block, LANES), BF16),
            pltpu.VMEM((n_tensor, block, LANES), BF16),
            pltpu.VMEM((segments, padded, LANES), F32),
            pltpu.VMEM((segments, padded, LANES), F32),
            pltpu.VMEM((n_tensor, 1, LANES), F32),
            pltpu.VMEM((n_tensor, 1, LANES), F32),
            pltpu.VMEM((n_dp, EXPERTS, LANES), F32),
            pltpu.VMEM((n_dp, EXPERTS, LANES), F32),
            pltpu.VMEM((LANES, LANES), F32),
            pltpu.VMEM((n_tensor, 1, LANES), F32),
            pltpu.VMEM((n_tensor, 1, LANES), F32),
            dma((3,)),
            dma((n_tensor,)),
            dma((n_tensor,)),
            dma,
            dma,
            dma,
            dma,
            dma,
            dma,
        ],
        compiler_params=pltpu.CompilerParams(
            collective_id=0, has_side_effects=True, vmem_limit_bytes=56 * 2**20
        ),
    )(
        expert_rows.reshape(slot_count, span),
        expert_ids.T,
        gate_logits.T,
        layer_input,
        out_grad,
    )
    chunks = 6
    slot_grad, logit_grad, router_grad = pl.pallas_call(
        functools.partial(hand_over, chunks),
        out_shape=(
            jax.ShapeDtypeStruct((slot_count, span), BF16),
            jax.ShapeDtypeStruct((2, tokens), F32),
            jax.ShapeDtypeStruct((owned, EXPERTS), F32),
        ),
        in_specs=[any_space] * 3,
        out_specs=(any_space,) * 3,
        scratch_shapes=[dma((chunks + 2,))],
        compiler_params=pltpu.CompilerParams(vmem_limit_bytes=2**20),
    )(slot_grad, logit_grad, router_grad)
    return slot_grad.reshape(expert_rows.shape), logit_grad.T, router_grad


def solution(mesh):
    in_specs = (
        P("dp", "tensor", None, None),
        P(("dp", "tensor"), None),
        P(("dp", "tensor"), None),
        P(("dp", "tensor"), None),
        P(("dp", "tensor"), None),
    )
    out_specs = (
        P("dp", "tensor", None, None),
        P(("dp", "tensor"), None),
        P(("dp", "tensor"), None),
    )
    return jax.shard_map(
        on_device, mesh=mesh, in_specs=in_specs, out_specs=out_specs, check_vma=False
    )
```

```python
import functools

import jax
import jax.numpy as jnp
from jax import lax
from jax.experimental import pallas as pl
from jax.experimental.pallas import tpu as pltpu
from jax.sharding import PartitionSpec as P

EXPERTS = 8
LANES = 128
F32 = jnp.float32
BF16 = jnp.bfloat16
MESH = pl.DeviceIdType.MESH


def iota(shape, axis):
    return lax.broadcasted_iota(jnp.int32, shape, axis)


def split3(x):
    hi = x.astype(BF16).astype(F32)
    mid = (x - hi).astype(BF16).astype(F32)
    return hi, mid, x - hi - mid


def wrapped(index, size):
    return jnp.where(index >= size, index - size, index)


def kernel(
    n_dp,
    n_tensor,
    scale,
    rows_hbm,
    ids_hbm,
    logits_hbm,
    input_hbm,
    grad_hbm,
    slot_out,
    logit_out,
    router_out,
    ids_ref,
    logits_ref,
    rows,
    inputs,
    grads,
    send,
    recv,
    rows32,
    slot32,
    mine_last,
    other_last,
    score_send,
    score_recv,
    term_send,
    term_recv,
    turned,
    part_send,
    part_recv,
    load_sem,
    send_sem,
    recv_sem,
    ssend_sem,
    srecv_sem,
    tsend_sem,
    trecv_sem,
    psend_sem,
    precv_sem,
    lsend_sem,
    lrecv_sem,
    fsend_sem,
    frecv_sem,
):
    me = lax.axis_index("tensor")
    group = lax.axis_index("dp")
    members = n_tensor // EXPERTS
    capacity = rows.shape[0] // n_tensor
    full = capacity - 1
    segments = rows.shape[1] // LANES
    body = full * segments
    tokens = grads.shape[0]

    barrier = pltpu.get_barrier_semaphore()

    def tensor_peer(i):
        return wrapped(me + i, n_tensor)

    def dp_peer(i):
        return wrapped(group + i, n_dp)

    load_ids = pltpu.make_async_copy(ids_hbm, ids_ref, load_sem.at[3])
    load_logits = pltpu.make_async_copy(logits_hbm, logits_ref, load_sem.at[4])
    load_grads = pltpu.make_async_copy(grad_hbm, grads, load_sem.at[0])
    load_rows = pltpu.make_async_copy(rows_hbm, rows, load_sem.at[1])
    load_inputs = pltpu.make_async_copy(input_hbm, inputs, load_sem.at[2])
    load_ids.start()
    load_logits.start()
    load_grads.start()

    @pl.loop(1, n_tensor, unroll=True)
    def _(i):
        pl.semaphore_signal(
            barrier, inc=1, device_id={"tensor": tensor_peer(i)}, device_id_type=MESH
        )

    @pl.loop(1, n_dp, unroll=True)
    def _(i):
        pl.semaphore_signal(barrier, inc=1, device_id={"dp": dp_peer(i)}, device_id_type=MESH)

    load_rows.start()
    load_inputs.start()
    load_ids.wait()
    load_logits.wait()

    id0, id1 = ids_ref[0:1, :], ids_ref[1:2, :]
    logit0, logit1 = logits_ref[0:1, :], logits_ref[1:2, :]
    prob0 = 1.0 / (1.0 + jnp.exp(logit1 - logit0))
    prob1 = 1.0 / (1.0 + jnp.exp(logit0 - logit1))
    experts = iota((EXPERTS, tokens), 0)
    hot0 = jnp.where(experts == id0, 1.0, 0.0)
    hot1 = jnp.where(experts == id1, 1.0, 0.0)
    earlier = jnp.where(
        iota((tokens, tokens), 0) < iota((tokens, tokens), 1), 1.0, 0.0
    ).astype(BF16)
    before = jnp.dot((hot0 + hot1).astype(BF16), earlier, preferred_element_type=F32)
    rank0 = jnp.sum(hot0 * before, axis=0, keepdims=True).astype(jnp.int32)
    rank1 = jnp.sum(hot1 * before, axis=0, keepdims=True).astype(jnp.int32)
    slots = iota((LANES, tokens), 0)
    tail_row = iota((16, LANES), 0)
    prob_row = 2 * segments

    load_grads.wait()
    pl.semaphore_wait(barrier, n_tensor - 1 + n_dp - 1)

    column, row, core = me // 8, lax.rem(me // 2, 4), lax.rem(me, 2)
    sibling = me + 1 - 2 * core
    tails = pl.ds(0, n_tensor // 2)
    main = pl.ds(0, body)
    last_tile = pl.ds(body, 16)

    def remote(source, target, sent, received, peer):
        return pltpu.make_async_remote_copy(
            src_ref=source,
            dst_ref=target,
            send_sem=sent,
            recv_sem=received,
            device_id={"tensor": peer},
            device_id_type=MESH,
        )

    def for_block(peer, act):
        @pl.when(lax.rem(peer, 2) == core)
        def _():
            act(remote(send.at[peer], recv.at[me], send_sem.at[peer], recv_sem.at[me], peer))

        @pl.when(lax.rem(peer, 2) != core)
        def _():
            act(
                remote(
                    send.at[peer, main],
                    recv.at[me, main],
                    send_sem.at[peer],
                    recv_sem.at[me],
                    peer,
                )
            )

    def start_block(peer):
        for_block(peer, lambda copy: copy.start())

    def sent_block(peer):
        for_block(peer, lambda copy: copy.wait_send())


    def partner(i, sign):
        part, place = i // 8, i - 8
        middle = (part == 1) | (part == 2)
        along_y = jnp.where(middle, 1 + 2 * lax.rem(i, 2), jnp.where(part == 0, 2, 0))
        rest = jnp.where(middle, place // 2, lax.rem(i, 8))
        along_x = lax.rem(rest // 2 + 1, 4)
        return (
            lax.rem(column + sign * along_x + 4, 4) * 8
            + lax.rem(row + sign * along_y + 4, 4) * 2
            + lax.rem(core + rest + 1, 2)
        )

    def pack(expert):
        key0 = jnp.where(id0 == expert, rank0, -1)
        key1 = jnp.where(id1 == expert, rank1, -1)
        placing = jnp.where((slots == key0) | (slots == key1), 1.0, 0.0).astype(BF16)
        prob = jnp.where(id0 == expert, prob0, jnp.where(id1 == expert, prob1, 0.0))
        hi, mid, lo = split3(prob)
        parts = jnp.where(
            tail_row == prob_row,
            hi,
            jnp.where(tail_row == prob_row + 1, mid, jnp.where(tail_row == prob_row + 2, lo, 0.0)),
        ).astype(BF16)
        slot_probs = lax.dot_general(
            parts, placing, (((1,), (1,)), ((), ())), preferred_element_type=F32
        )
        for k in range(members):
            peer = expert * members + k
            packed = jnp.dot(
                placing[: full + 16],
                grads[:, k * segments * LANES : (k + 1) * segments * LANES],
                preferred_element_type=F32,
            )
            if k % 2 == 0:
                tail = slot_probs
            for j in range(segments):
                piece = packed[:, j * LANES : (j + 1) * LANES]
                send[peer, j * full : (j + 1) * full, :] = piece[:full].astype(BF16)
                place = k % 2 * segments + j
                tail = jnp.where(tail_row == place, piece[full : full + 1], tail)
            if k % 2 == 1:
                send[peer - 1 + core, body : body + 16, :] = tail.astype(BF16)

    half = row // 2

    @pl.loop(0, 4)
    def _(i):
        pack(lax.rem(column + i + 1, 4) * 2 + 1 - half)
        start_block(partner(2 * i, 1))
        start_block(partner(2 * i + 1, 1))

    @pl.loop(0, 4)
    def _(i):
        pack(lax.rem(column + i + 1, 4) * 2 + half)

    @pl.loop(24, n_tensor - 1)
    def _(i):
        start_block(partner(i, 1))

    pltpu.make_async_copy(send.at[me], recv.at[me], recv_sem.at[me]).start()

    @pl.loop(8, 24)
    def _(i):
        start_block(partner(i, 1))

    load_rows.wait()

    @pl.loop(0, rows.shape[0] // 32)
    def _(i):
        at = pl.multiple_of(i * 32, 32)
        for j in range(segments):
            rows32[j, pl.ds(at, 32), :] = rows[
                pl.ds(at, 32), j * LANES : (j + 1) * LANES
            ].astype(F32)

    line_row = iota((8, LANES), 0)

    @pl.loop(0, n_tensor)
    def _(i):
        tile = jnp.zeros((8, LANES), F32)
        for j in range(segments):
            tile = jnp.where(line_row == j, rows32[j, pl.ds(i * capacity + full, 1), :], tile)
        mine_last[i] = tile

    exchange = remote(mine_last, other_last, lsend_sem, lrecv_sem, sibling)
    exchange.start()

    diagonal = iota((full, LANES), 0) == iota((full, LANES), 1)
    lane = iota((1, LANES), 1)

    def remote_scores(index, peer):
        return pltpu.make_async_remote_copy(
            src_ref=score_send.at[peer],
            dst_ref=score_recv.at[index],
            send_sem=ssend_sem,
            recv_sem=srecv_sem,
            device_id={"tensor": peer},
            device_id_type=MESH,
        )

    exchange.wait_recv()

    @pl.loop(0, n_tensor)
    def _(i):
        source = partner(lax.rem(i + 24, n_tensor), -1)
        same = lax.rem(source, 2) == core

        @pl.when(same)
        def _():
            pltpu.make_async_copy(send.at[source], recv.at[source], recv_sem.at[source]).wait()

        @pl.when(lax.rem(source, 2) != core)
        def _():
            pltpu.make_async_copy(
                send.at[source, main], recv.at[source, main], recv_sem.at[source]
            ).wait()

        at = source * capacity
        products = jnp.zeros((full, LANES), F32)
        for j in range(segments):
            piece = recv[source, j * full : (j + 1) * full, :].astype(F32)
            products += piece * rows32[j, pl.ds(at, full), :]
        sums = jnp.sum(products, axis=1, keepdims=True)
        line = jnp.sum(jnp.where(diagonal, sums, 0.0), axis=0, keepdims=True)
        score_send[source] = line

        @pl.when(same)
        def _():
            remote(
                recv.at[source, last_tile],
                recv.at[source, last_tile],
                fsend_sem,
                frecv_sem,
                sibling,
            ).start()
            tail = recv[source, body : body + 16, :].astype(F32)
            mine, other = mine_last[source], other_last[source]
            first = jnp.where(core == 0, mine, other)
            second = jnp.where(core == 0, other, mine)
            last = tail[:8] * first + tail[segments : segments + 8] * second
            last_sum = jnp.sum(jnp.sum(last, axis=0, keepdims=True), axis=1, keepdims=True)
            score_send[source] = jnp.where(lane == full, last_sum, line)

        @pl.when(source != me)
        def _():
            remote_scores(me, source).start()

        @pl.when(source == me)
        def _():
            pltpu.make_async_copy(
                score_send.at[me], score_recv.at[me], srecv_sem
            ).start()

    ranks = iota((LANES, tokens), 0)
    chosen0 = jnp.where(ranks == rank0, 1.0, 0.0).astype(BF16)
    chosen1 = jnp.where(ranks == rank1, 1.0, 0.0).astype(BF16)
    load_inputs.wait()

    pltpu.make_async_copy(score_send, score_recv, srecv_sem).wait()
    scores = jnp.zeros((EXPERTS, LANES), F32)
    for expert in range(EXPERTS):
        total = score_recv[expert * members]
        for k in range(1, members):
            total += score_recv[expert * members + k]
        scores = jnp.where(iota((EXPERTS, LANES), 0) == expert, total, scores)
    hi, mid, lo = split3(scores)
    terms = jnp.concatenate([hi, mid, lo, jnp.zeros_like(lo)], axis=0).astype(BF16)

    def looked_up(chosen, hot):
        found = jnp.dot(terms, chosen, preferred_element_type=F32)
        found = found[:EXPERTS] + found[EXPERTS : 2 * EXPERTS] + found[2 * EXPERTS : 3 * EXPERTS]
        return jnp.sum(found * hot, axis=0, keepdims=True)

    score0 = looked_up(chosen0, hot0)
    score1 = looked_up(chosen1, hot1)
    average = prob0 * score0 + prob1 * score1
    slope0 = prob0 * (score0 - average)
    slope1 = prob1 * (score1 - average)
    logit_out[0:1, :] = slope0
    logit_out[1:2, :] = slope1
    combined = (hot0 * slope0 + hot1 * slope1).astype(BF16)

    def remote_term(index, peer):
        return pltpu.make_async_remote_copy(
            src_ref=term_send.at[peer],
            dst_ref=term_recv.at[index],
            send_sem=tsend_sem,
            recv_sem=trecv_sem,
            device_id={"dp": peer},
            device_id_type=MESH,
        )

    for k in range(members):
        term = jnp.dot(
            combined,
            inputs[:, k * segments * LANES : (k + 1) * segments * LANES],
            preferred_element_type=F32,
        )
        for j in range(segments):
            term_send[k * segments + j] = term[:, j * LANES : (j + 1) * LANES]

    @pl.loop(1, n_dp, unroll=True)
    def _(i):
        remote_term(group, dp_peer(i)).start()

    own_term = pltpu.make_async_copy(
        term_send.at[group], term_recv.at[group], trecv_sem
    )
    own_term.start()

    pltpu.make_async_copy(send.at[tails, last_tile], recv.at[tails, last_tile], frecv_sem).wait()

    @pl.loop(0, n_tensor)
    def _(i):
        at = i * capacity
        tail = recv[i, body : body + 16, :].astype(F32)
        prob = (
            tail[prob_row : prob_row + 1]
            + tail[prob_row + 1 : prob_row + 2]
            + tail[prob_row + 2 : prob_row + 3]
        )
        prob_column = jnp.sum(jnp.where(diagonal, prob, 0.0), axis=1, keepdims=True)
        prob_last = jnp.sum(jnp.where(lane == full, prob, 0.0), axis=1, keepdims=True)
        lasts = jnp.where(core == 0, tail[:8], tail[segments : segments + 8]) * prob_last
        for j in range(segments):
            piece = recv[i, j * full : (j + 1) * full, :].astype(F32)
            slot32[j, pl.ds(at, full), :] = piece * prob_column
            slot32[j, pl.ds(at + full, 1), :] = lasts[j : j + 1]

    @pl.loop(0, rows.shape[0] // 32)
    def _(i):
        at = pl.multiple_of(i * 32, 32)
        for j in range(segments):
            slot_out[pl.ds(at, 32), j * LANES : (j + 1) * LANES] = slot32[
                j, pl.ds(at, 32), :
            ].astype(BF16)

    pltpu.make_async_copy(term_send, term_recv, trecv_sem).wait()
    total = term_recv[0]
    for g in range(1, n_dp):
        total += term_recv[g]

    square = jnp.concatenate([total, jnp.zeros((LANES - EXPERTS, LANES), F32)], axis=0)
    turned[...] = jnp.transpose(square)
    owned = LANES // n_tensor
    lines = turned[pl.ds(0, n_tensor, stride=owned), :]
    for j in range(1, owned):
        lines += pltpu.roll(turned[pl.ds(j, n_tensor, stride=owned), :], j * EXPERTS, 1)
    for i in range(n_tensor):
        part_send[i] = lines[i : i + 1]

    def remote_part(index, peer):
        return pltpu.make_async_remote_copy(
            src_ref=part_send.at[peer],
            dst_ref=part_recv.at[index],
            send_sem=psend_sem,
            recv_sem=precv_sem,
            device_id={"tensor": peer},
            device_id_type=MESH,
        )

    @pl.loop(1, n_tensor, unroll=True)
    def _(i):
        remote_part(me, tensor_peer(i)).start()

    own_part = pltpu.make_async_copy(part_send.at[me], part_recv.at[me], precv_sem)
    own_part.start()

    @pl.loop(1, n_tensor)
    def _(i):
        sent_block(tensor_peer(i))

    remote(mine_last, other_last, lsend_sem, lrecv_sem, sibling).wait_send()
    pltpu.make_async_copy(
        send.at[tails, last_tile], recv.at[tails, last_tile], fsend_sem
    ).wait()

    others = pl.ds(0, n_tensor - 1)
    pltpu.make_async_copy(score_send.at[others], score_recv.at[others], ssend_sem).wait()
    others_dp = pl.ds(0, n_dp - 1)
    pltpu.make_async_copy(term_send.at[others_dp], term_recv.at[others_dp], tsend_sem).wait()

    pltpu.make_async_copy(part_send, part_recv, precv_sem).wait()
    line = part_recv[0]
    for i in range(1, n_tensor):
        line += part_recv[i]
    line = line * scale
    for j in range(owned):
        router_out[j : j + 1, :] = line[:, j * EXPERTS : (j + 1) * EXPERTS]

    pltpu.make_async_copy(part_send.at[others], part_recv.at[others], psend_sem).wait()


def hand_over(chunks, slots, logits, router, slots_out, logits_out, router_out, sem):
    rows = slots.shape[0] // chunks
    parts = [pl.ds(i * rows, rows) for i in range(chunks)]
    copies = [
        pltpu.make_async_copy(slots.at[part], slots_out.at[part], sem.at[i])
        for i, part in enumerate(parts)
    ]
    copies.append(pltpu.make_async_copy(logits, logits_out, sem.at[chunks]))
    copies.append(pltpu.make_async_copy(router, router_out, sem.at[chunks + 1]))
    for copy in copies:
        copy.start()
    for copy in copies:
        copy.wait()


def on_device(expert_rows, expert_ids, gate_logits, layer_input, out_grad):
    n_tensor = lax.axis_size("tensor")
    n_dp = lax.axis_size("dp")
    slot_count, span = expert_rows.shape[2:]
    tokens, width = out_grad.shape
    capacity = slot_count // n_tensor
    segments = span // LANES
    block = (capacity - 1) * segments + 16
    owned = width // (n_dp * n_tensor)
    padded = slot_count + 8
    any_space = pl.BlockSpec(memory_space=pl.ANY)
    in_vmem = pl.BlockSpec(memory_space=pltpu.VMEM)
    dma = pltpu.SemaphoreType.DMA
    slot_grad, logit_grad, router_grad = pl.pallas_call(
        functools.partial(kernel, n_dp, n_tensor, (tokens * n_dp * n_tensor) ** -0.5),
        out_shape=(
            pltpu.VMEM((slot_count, span), BF16),
            pltpu.VMEM((2, tokens), F32),
            pltpu.VMEM((owned, EXPERTS), F32),
        ),
        in_specs=[any_space] * 5,
        out_specs=(in_vmem, in_vmem, in_vmem),
        scratch_shapes=[
            pltpu.VMEM((2, tokens), jnp.int32),
            pltpu.VMEM((2, tokens), F32),
            pltpu.VMEM((slot_count, span), BF16),
            pltpu.VMEM((tokens, width), BF16),
            pltpu.VMEM((tokens, width), BF16),
            pltpu.VMEM((n_tensor, block, LANES), BF16),
            pltpu.VMEM((n_tensor, block, LANES), BF16),
            pltpu.VMEM((segments, padded, LANES), F32),
            pltpu.VMEM((segments, padded, LANES), F32),
            pltpu.VMEM((n_tensor, 8, LANES), F32),
            pltpu.VMEM((n_tensor, 8, LANES), F32),
            pltpu.VMEM((n_tensor, 1, LANES), F32),
            pltpu.VMEM((n_tensor, 1, LANES), F32),
            pltpu.VMEM((n_dp, EXPERTS, LANES), F32),
            pltpu.VMEM((n_dp, EXPERTS, LANES), F32),
            pltpu.VMEM((LANES, LANES), F32),
            pltpu.VMEM((n_tensor, 1, LANES), F32),
            pltpu.VMEM((n_tensor, 1, LANES), F32),
            dma((5,)),
            dma((n_tensor,)),
            dma((n_tensor,)),
            dma,
            dma,
            dma,
            dma,
            dma,
            dma,
            dma,
            dma,
            dma,
            dma,
        ],
        compiler_params=pltpu.CompilerParams(
            collective_id=0, has_side_effects=True, vmem_limit_bytes=56 * 2**20
        ),
    )(
        expert_rows.reshape(slot_count, span),
        expert_ids.T,
        gate_logits.T,
        layer_input,
        out_grad,
    )
    chunks = 6
    slot_grad, logit_grad, router_grad = pl.pallas_call(
        functools.partial(hand_over, chunks),
        out_shape=(
            jax.ShapeDtypeStruct((slot_count, span), BF16),
            jax.ShapeDtypeStruct((2, tokens), F32),
            jax.ShapeDtypeStruct((owned, EXPERTS), F32),
        ),
        in_specs=[any_space] * 3,
        out_specs=(any_space,) * 3,
        scratch_shapes=[dma((chunks + 2,))],
        compiler_params=pltpu.CompilerParams(vmem_limit_bytes=2**20),
    )(slot_grad, logit_grad, router_grad)
    return slot_grad.reshape(expert_rows.shape), logit_grad.T, router_grad


def solution(mesh):
    in_specs = (
        P("dp", "tensor", None, None),
        P(("dp", "tensor"), None),
        P(("dp", "tensor"), None),
        P(("dp", "tensor"), None),
        P(("dp", "tensor"), None),
    )
    out_specs = (
        P("dp", "tensor", None, None),
        P(("dp", "tensor"), None),
        P(("dp", "tensor"), None),
    )
    return jax.shard_map(
        on_device, mesh=mesh, in_specs=in_specs, out_specs=out_specs, check_vma=False
    )
```

```python
import functools

import jax
import jax.numpy as jnp
from jax import lax
from jax.experimental import pallas as pl
from jax.experimental.pallas import tpu as pltpu
from jax.sharding import PartitionSpec as P

EXPERTS = 8
LANES = 128
F32 = jnp.float32
BF16 = jnp.bfloat16
MESH = pl.DeviceIdType.MESH


def iota(shape, axis):
    return lax.broadcasted_iota(jnp.int32, shape, axis)


def split3(x):
    hi = x.astype(BF16).astype(F32)
    mid = (x - hi).astype(BF16).astype(F32)
    return hi, mid, x - hi - mid


def summed(parts):
    while len(parts) > 1:
        pairs = [a + b for a, b in zip(parts[::2], parts[1::2])]
        parts = pairs + parts[len(pairs) * 2 :]
    return parts[0]


def wrapped(index, size):
    return jnp.where(index >= size, index - size, index)


def kernel(
    n_dp,
    n_tensor,
    scale,
    rows_hbm,
    ids_hbm,
    logits_hbm,
    input_hbm,
    grad_hbm,
    slot_out,
    logit_out,
    router_out,
    ids_ref,
    logits_ref,
    rows,
    inputs,
    grads,
    send,
    recv,
    rows32,
    slot32,
    mine_last,
    other_last,
    score_send,
    score_recv,
    term_send,
    term_recv,
    turned,
    part_send,
    part_recv,
    load_sem,
    send_sem,
    recv_sem,
    ssend_sem,
    srecv_sem,
    tsend_sem,
    trecv_sem,
    psend_sem,
    precv_sem,
    lsend_sem,
    lrecv_sem,
    fsend_sem,
    frecv_sem,
):
    me = lax.axis_index("tensor")
    group = lax.axis_index("dp")
    members = n_tensor // EXPERTS
    capacity = rows.shape[0] // n_tensor
    full = capacity - 1
    segments = rows.shape[1] // LANES
    body = full * segments
    tokens = grads.shape[0]

    barrier = pltpu.get_barrier_semaphore()

    def tensor_peer(i):
        return wrapped(me + i, n_tensor)

    def dp_peer(i):
        return wrapped(group + i, n_dp)

    column, row, core = me // 8, lax.rem(me // 2, 4), lax.rem(me, 2)

    def partner(i, sign):
        part, place = i // 8, i - 8
        middle = (part == 1) | (part == 2)
        along_y = jnp.where(middle, 1 + 2 * lax.rem(i, 2), jnp.where(part == 0, 2, 0))
        rest = jnp.where(middle, place // 2, lax.rem(i, 8))
        along_x = lax.rem(rest // 2 + 1, 4)
        return (
            lax.rem(column + sign * along_x + 4, 4) * 8
            + lax.rem(row + sign * along_y + 4, 4) * 2
            + lax.rem(core + rest + 1, 2)
        )

    load_ids = pltpu.make_async_copy(ids_hbm, ids_ref, load_sem.at[3])
    load_logits = pltpu.make_async_copy(logits_hbm, logits_ref, load_sem.at[4])
    load_grads = pltpu.make_async_copy(grad_hbm, grads, load_sem.at[0])
    load_rows = pltpu.make_async_copy(rows_hbm, rows, load_sem.at[1])
    load_inputs = pltpu.make_async_copy(input_hbm, inputs, load_sem.at[2])
    load_ids.start()
    load_logits.start()
    load_grads.start()

    for i in range(n_tensor - 1):
        pl.semaphore_signal(
            barrier, inc=1, device_id={"tensor": partner(i, 1)}, device_id_type=MESH
        )

    @pl.loop(1, n_dp, unroll=True)
    def _(i):
        pl.semaphore_signal(barrier, inc=1, device_id={"dp": dp_peer(i)}, device_id_type=MESH)

    load_rows.start()
    load_inputs.start()
    load_ids.wait()
    load_logits.wait()

    id0, id1 = ids_ref[0:1, :], ids_ref[1:2, :]
    logit0, logit1 = logits_ref[0:1, :], logits_ref[1:2, :]
    prob0 = 1.0 / (1.0 + jnp.exp(logit1 - logit0))
    prob1 = 1.0 / (1.0 + jnp.exp(logit0 - logit1))
    experts = iota((EXPERTS, tokens), 0)
    hot0 = jnp.where(experts == id0, 1.0, 0.0)
    hot1 = jnp.where(experts == id1, 1.0, 0.0)
    earlier = jnp.where(
        iota((tokens, tokens), 0) < iota((tokens, tokens), 1), 1.0, 0.0
    ).astype(BF16)
    before = jnp.dot((hot0 + hot1).astype(BF16), earlier, preferred_element_type=F32)
    rank0 = jnp.sum(hot0 * before, axis=0, keepdims=True).astype(jnp.int32)
    rank1 = jnp.sum(hot1 * before, axis=0, keepdims=True).astype(jnp.int32)
    slots = iota((LANES, tokens), 0)
    tail_row = iota((16, LANES), 0)
    prob_row = 2 * segments

    load_grads.wait()
    pl.semaphore_wait(barrier, n_tensor - 1 + n_dp - 1)

    sibling = me + 1 - 2 * core
    tails = pl.ds(0, n_tensor // 2)
    main = pl.ds(0, body)
    last_tile = pl.ds(body, 16)

    def remote(source, target, sent, received, peer):
        return pltpu.make_async_remote_copy(
            src_ref=source,
            dst_ref=target,
            send_sem=sent,
            recv_sem=received,
            device_id={"tensor": peer},
            device_id_type=MESH,
        )

    def for_block(peer, act):
        @pl.when(lax.rem(peer, 2) == core)
        def _():
            act(remote(send.at[peer], recv.at[me], send_sem.at[peer], recv_sem.at[me], peer))

        @pl.when(lax.rem(peer, 2) != core)
        def _():
            act(
                remote(
                    send.at[peer, main],
                    recv.at[me, main],
                    send_sem.at[peer],
                    recv_sem.at[me],
                    peer,
                )
            )

    def start_block(peer):
        for_block(peer, lambda copy: copy.start())

    def sent_block(peer):
        for_block(peer, lambda copy: copy.wait_send())


    def pack(expert):
        key0 = jnp.where(id0 == expert, rank0, -1)
        key1 = jnp.where(id1 == expert, rank1, -1)
        placing = jnp.where((slots == key0) | (slots == key1), 1.0, 0.0).astype(BF16)
        prob = jnp.where(id0 == expert, prob0, jnp.where(id1 == expert, prob1, 0.0))
        hi, mid, lo = split3(prob)
        parts = jnp.where(
            tail_row == prob_row,
            hi,
            jnp.where(tail_row == prob_row + 1, mid, jnp.where(tail_row == prob_row + 2, lo, 0.0)),
        ).astype(BF16)
        slot_probs = lax.dot_general(
            parts, placing, (((1,), (1,)), ((), ())), preferred_element_type=F32
        )
        for k in range(members):
            peer = expert * members + k
            packed = jnp.dot(
                placing[: full + 16],
                grads[:, k * segments * LANES : (k + 1) * segments * LANES],
                preferred_element_type=F32,
            )
            if k % 2 == 0:
                tail = slot_probs
            for j in range(segments):
                piece = packed[:, j * LANES : (j + 1) * LANES]
                send[peer, j * full : (j + 1) * full, :] = piece[:full].astype(BF16)
                place = k % 2 * segments + j
                tail = jnp.where(tail_row == place, piece[full : full + 1], tail)
            if k % 2 == 1:
                send[peer - 1 + core, body : body + 16, :] = tail.astype(BF16)

    half = row // 2

    @pl.loop(0, 4)
    def _(i):
        pack(lax.rem(column + i + 1, 4) * 2 + 1 - half)
        start_block(partner(2 * i, 1))
        start_block(partner(2 * i + 1, 1))

    @pl.loop(0, 4)
    def _(i):
        pack(lax.rem(column + i + 1, 4) * 2 + half)

    @pl.loop(24, n_tensor - 1)
    def _(i):
        start_block(partner(i, 1))

    pltpu.make_async_copy(send.at[me], recv.at[me], recv_sem.at[me]).start()

    @pl.loop(8, 24)
    def _(i):
        start_block(partner(i, 1))

    load_rows.wait()

    @pl.loop(0, rows.shape[0] // 32)
    def _(i):
        at = pl.multiple_of(i * 32, 32)
        for j in range(segments):
            rows32[j, pl.ds(at, 32), :] = rows[
                pl.ds(at, 32), j * LANES : (j + 1) * LANES
            ].astype(F32)

    line_row = iota((8, LANES), 0)

    @pl.loop(0, n_tensor)
    def _(i):
        tile = jnp.zeros((8, LANES), F32)
        for j in range(segments):
            tile = jnp.where(line_row == j, rows32[j, pl.ds(i * capacity + full, 1), :], tile)
        mine_last[i] = tile

    exchange = remote(mine_last, other_last, lsend_sem, lrecv_sem, sibling)
    exchange.start()

    diagonal = iota((full, LANES), 0) == iota((full, LANES), 1)
    lane = iota((1, LANES), 1)

    def remote_scores(index, peer):
        return pltpu.make_async_remote_copy(
            src_ref=score_send.at[peer],
            dst_ref=score_recv.at[index],
            send_sem=ssend_sem,
            recv_sem=srecv_sem,
            device_id={"tensor": peer},
            device_id_type=MESH,
        )

    exchange.wait_recv()

    @pl.loop(0, n_tensor)
    def _(i):
        source = partner(lax.rem(i + 24, n_tensor), -1)
        same = lax.rem(source, 2) == core

        @pl.when(same)
        def _():
            pltpu.make_async_copy(send.at[source], recv.at[source], recv_sem.at[source]).wait()

        @pl.when(lax.rem(source, 2) != core)
        def _():
            pltpu.make_async_copy(
                send.at[source, main], recv.at[source, main], recv_sem.at[source]
            ).wait()

        at = source * capacity
        products = jnp.zeros((full, LANES), F32)
        for j in range(segments):
            piece = recv[source, j * full : (j + 1) * full, :].astype(F32)
            products += piece * rows32[j, pl.ds(at, full), :]
        sums = jnp.sum(products, axis=1, keepdims=True)
        line = jnp.sum(jnp.where(diagonal, sums, 0.0), axis=0, keepdims=True)
        score_send[source] = line

        @pl.when(same)
        def _():
            remote(
                recv.at[source, last_tile],
                recv.at[source, last_tile],
                fsend_sem,
                frecv_sem,
                sibling,
            ).start()
            tail = recv[source, body : body + 16, :].astype(F32)
            mine, other = mine_last[source], other_last[source]
            first = jnp.where(core == 0, mine, other)
            second = jnp.where(core == 0, other, mine)
            last = tail[:8] * first + tail[segments : segments + 8] * second
            last_sum = jnp.sum(jnp.sum(last, axis=0, keepdims=True), axis=1, keepdims=True)
            score_send[source] = jnp.where(lane == full, last_sum, line)

        @pl.when(source != me)
        def _():
            remote_scores(me, source).start()

        @pl.when(source == me)
        def _():
            pltpu.make_async_copy(
                score_send.at[me], score_recv.at[me], srecv_sem
            ).start()

    ranks = iota((LANES, tokens), 0)
    chosen0 = jnp.where(ranks == rank0, 1.0, 0.0).astype(BF16)
    chosen1 = jnp.where(ranks == rank1, 1.0, 0.0).astype(BF16)
    load_inputs.wait()

    pltpu.make_async_copy(score_send, score_recv, srecv_sem).wait()
    scores = jnp.zeros((EXPERTS, LANES), F32)
    for expert in range(EXPERTS):
        total = score_recv[expert * members]
        for k in range(1, members):
            total += score_recv[expert * members + k]
        scores = jnp.where(iota((EXPERTS, LANES), 0) == expert, total, scores)
    hi, mid, lo = split3(scores)
    terms = jnp.concatenate([hi, mid, lo, jnp.zeros_like(lo)], axis=0).astype(BF16)

    def looked_up(chosen, hot):
        found = jnp.dot(terms, chosen, preferred_element_type=F32)
        found = found[:EXPERTS] + found[EXPERTS : 2 * EXPERTS] + found[2 * EXPERTS : 3 * EXPERTS]
        return jnp.sum(found * hot, axis=0, keepdims=True)

    score0 = looked_up(chosen0, hot0)
    score1 = looked_up(chosen1, hot1)
    average = prob0 * score0 + prob1 * score1
    slope0 = prob0 * (score0 - average)
    slope1 = prob1 * (score1 - average)
    logit_out[0:1, :] = slope0
    logit_out[1:2, :] = slope1
    combined = (hot0 * slope0 + hot1 * slope1).astype(BF16)

    def remote_term(index, peer):
        return pltpu.make_async_remote_copy(
            src_ref=term_send.at[peer],
            dst_ref=term_recv.at[index],
            send_sem=tsend_sem,
            recv_sem=trecv_sem,
            device_id={"dp": peer},
            device_id_type=MESH,
        )

    def remote_term(index, peer):
        return pltpu.make_async_remote_copy(
            src_ref=term_send.at[peer],
            dst_ref=term_recv.at[index],
            send_sem=tsend_sem,
            recv_sem=trecv_sem,
            device_id={"dp": peer},
            device_id_type=MESH,
        )

    for k in range(members):
        term = jnp.dot(
            combined,
            inputs[:, k * segments * LANES : (k + 1) * segments * LANES],
            preferred_element_type=F32,
        )
        for j in range(segments):
            term_send[k * segments + j] = term[:, j * LANES : (j + 1) * LANES]

    for k in range(members):
        term = jnp.dot(
            combined,
            inputs[:, k * segments * LANES : (k + 1) * segments * LANES],
            preferred_element_type=F32,
        )
        for j in range(segments):
            term_send[k * segments + j] = term[:, j * LANES : (j + 1) * LANES]
        for j in range(segments):
            peer = k * segments + j

            @pl.when(group != peer)
            def _(peer=peer):
                remote_term(group, peer).start()

    own_term = pltpu.make_async_copy(
        term_send.at[group], term_recv.at[group], trecv_sem
    )
    own_term.start()

    pltpu.make_async_copy(send.at[tails, last_tile], recv.at[tails, last_tile], frecv_sem).wait()

    @pl.loop(0, n_tensor)
    def _(i):
        at = i * capacity
        tail = recv[i, body : body + 16, :].astype(F32)
        prob = (
            tail[prob_row : prob_row + 1]
            + tail[prob_row + 1 : prob_row + 2]
            + tail[prob_row + 2 : prob_row + 3]
        )
        prob_column = jnp.sum(jnp.where(diagonal, prob, 0.0), axis=1, keepdims=True)
        prob_last = jnp.sum(jnp.where(lane == full, prob, 0.0), axis=1, keepdims=True)
        lasts = jnp.where(core == 0, tail[:8], tail[segments : segments + 8]) * prob_last
        for j in range(segments):
            piece = recv[i, j * full : (j + 1) * full, :].astype(F32)
            slot32[j, pl.ds(at, full), :] = piece * prob_column
            slot32[j, pl.ds(at + full, 1), :] = lasts[j : j + 1]

    @pl.loop(0, rows.shape[0] // 32)
    def _(i):
        at = pl.multiple_of(i * 32, 32)
        for j in range(segments):
            slot_out[pl.ds(at, 32), j * LANES : (j + 1) * LANES] = slot32[
                j, pl.ds(at, 32), :
            ].astype(BF16)

    pltpu.make_async_copy(term_send, term_recv, trecv_sem).wait()
    total = summed([term_recv[g] for g in range(n_dp)])

    square = jnp.concatenate([total, jnp.zeros((LANES - EXPERTS, LANES), F32)], axis=0)
    turned[...] = jnp.transpose(square)
    owned = LANES // n_tensor
    lines = turned[pl.ds(0, n_tensor, stride=owned), :]
    for j in range(1, owned):
        lines += pltpu.roll(turned[pl.ds(j, n_tensor, stride=owned), :], j * EXPERTS, 1)
    for i in range(n_tensor):
        part_send[i] = lines[i : i + 1]

    def remote_part(index, peer):
        return pltpu.make_async_remote_copy(
            src_ref=part_send.at[peer],
            dst_ref=part_recv.at[index],
            send_sem=psend_sem,
            recv_sem=precv_sem,
            device_id={"tensor": peer},
            device_id_type=MESH,
        )

    @pl.loop(1, n_tensor, unroll=True)
    def _(i):
        remote_part(me, tensor_peer(i)).start()

    own_part = pltpu.make_async_copy(part_send.at[me], part_recv.at[me], precv_sem)
    own_part.start()

    @pl.loop(1, n_tensor)
    def _(i):
        sent_block(tensor_peer(i))

    remote(mine_last, other_last, lsend_sem, lrecv_sem, sibling).wait_send()
    pltpu.make_async_copy(
        send.at[tails, last_tile], recv.at[tails, last_tile], fsend_sem
    ).wait()

    others = pl.ds(0, n_tensor - 1)
    pltpu.make_async_copy(score_send.at[others], score_recv.at[others], ssend_sem).wait()
    others_dp = pl.ds(0, n_dp - 1)
    pltpu.make_async_copy(term_send.at[others_dp], term_recv.at[others_dp], tsend_sem).wait()

    pltpu.make_async_copy(part_send, part_recv, precv_sem).wait()
    line = summed([part_recv[i] for i in range(n_tensor)]) * scale
    for j in range(owned):
        router_out[j : j + 1, :] = line[:, j * EXPERTS : (j + 1) * EXPERTS]

    pltpu.make_async_copy(part_send.at[others], part_recv.at[others], psend_sem).wait()


def hand_over(chunks, slots, logits, router, slots_out, logits_out, router_out, sem):
    rows = slots.shape[0] // chunks
    parts = [pl.ds(i * rows, rows) for i in range(chunks)]
    copies = [
        pltpu.make_async_copy(slots.at[part], slots_out.at[part], sem.at[i])
        for i, part in enumerate(parts)
    ]
    copies.append(pltpu.make_async_copy(logits, logits_out, sem.at[chunks]))
    copies.append(pltpu.make_async_copy(router, router_out, sem.at[chunks + 1]))
    for copy in copies:
        copy.start()
    for copy in copies:
        copy.wait()


def on_device(expert_rows, expert_ids, gate_logits, layer_input, out_grad):
    n_tensor = lax.axis_size("tensor")
    n_dp = lax.axis_size("dp")
    slot_count, span = expert_rows.shape[2:]
    tokens, width = out_grad.shape
    capacity = slot_count // n_tensor
    segments = span // LANES
    block = (capacity - 1) * segments + 16
    owned = width // (n_dp * n_tensor)
    padded = slot_count + 8
    any_space = pl.BlockSpec(memory_space=pl.ANY)
    in_vmem = pl.BlockSpec(memory_space=pltpu.VMEM)
    dma = pltpu.SemaphoreType.DMA
    slot_grad, logit_grad, router_grad = pl.pallas_call(
        functools.partial(kernel, n_dp, n_tensor, (tokens * n_dp * n_tensor) ** -0.5),
        out_shape=(
            pltpu.VMEM((slot_count, span), BF16),
            pltpu.VMEM((2, tokens), F32),
            pltpu.VMEM((owned, EXPERTS), F32),
        ),
        in_specs=[any_space] * 5,
        out_specs=(in_vmem, in_vmem, in_vmem),
        scratch_shapes=[
            pltpu.VMEM((2, tokens), jnp.int32),
            pltpu.VMEM((2, tokens), F32),
            pltpu.VMEM((slot_count, span), BF16),
            pltpu.VMEM((tokens, width), BF16),
            pltpu.VMEM((tokens, width), BF16),
            pltpu.VMEM((n_tensor, block, LANES), BF16),
            pltpu.VMEM((n_tensor, block, LANES), BF16),
            pltpu.VMEM((segments, padded, LANES), F32),
            pltpu.VMEM((segments, padded, LANES), F32),
            pltpu.VMEM((n_tensor, 8, LANES), F32),
            pltpu.VMEM((n_tensor, 8, LANES), F32),
            pltpu.VMEM((n_tensor, 1, LANES), F32),
            pltpu.VMEM((n_tensor, 1, LANES), F32),
            pltpu.VMEM((n_dp, EXPERTS, LANES), F32),
            pltpu.VMEM((n_dp, EXPERTS, LANES), F32),
            pltpu.VMEM((LANES, LANES), F32),
            pltpu.VMEM((n_tensor, 1, LANES), F32),
            pltpu.VMEM((n_tensor, 1, LANES), F32),
            dma((5,)),
            dma((n_tensor,)),
            dma((n_tensor,)),
            dma,
            dma,
            dma,
            dma,
            dma,
            dma,
            dma,
            dma,
            dma,
            dma,
        ],
        compiler_params=pltpu.CompilerParams(
            collective_id=0, has_side_effects=True, vmem_limit_bytes=56 * 2**20
        ),
    )(
        expert_rows.reshape(slot_count, span),
        expert_ids.T,
        gate_logits.T,
        layer_input,
        out_grad,
    )
    chunks = 6
    slot_grad, logit_grad, router_grad = pl.pallas_call(
        functools.partial(hand_over, chunks),
        out_shape=(
            jax.ShapeDtypeStruct((slot_count, span), BF16),
            jax.ShapeDtypeStruct((2, tokens), F32),
            jax.ShapeDtypeStruct((owned, EXPERTS), F32),
        ),
        in_specs=[any_space] * 3,
        out_specs=(any_space,) * 3,
        scratch_shapes=[dma((chunks + 2,))],
        compiler_params=pltpu.CompilerParams(vmem_limit_bytes=2**20),
    )(slot_grad, logit_grad, router_grad)
    return slot_grad.reshape(expert_rows.shape), logit_grad.T, router_grad


def solution(mesh):
    in_specs = (
        P("dp", "tensor", None, None),
        P(("dp", "tensor"), None),
        P(("dp", "tensor"), None),
        P(("dp", "tensor"), None),
        P(("dp", "tensor"), None),
    )
    out_specs = (
        P("dp", "tensor", None, None),
        P(("dp", "tensor"), None),
        P(("dp", "tensor"), None),
    )
    return jax.shard_map(
        on_device, mesh=mesh, in_specs=in_specs, out_specs=out_specs, check_vma=False
    )
```

```python
import functools

import jax
import jax.numpy as jnp
from jax import lax
from jax.experimental import pallas as pl
from jax.experimental.pallas import tpu as pltpu
from jax.sharding import PartitionSpec as P

EXPERTS = 8
LANES = 128
F32 = jnp.float32
BF16 = jnp.bfloat16
MESH = pl.DeviceIdType.MESH


def iota(shape, axis):
    return lax.broadcasted_iota(jnp.int32, shape, axis)


def split3(x):
    hi = x.astype(BF16).astype(F32)
    mid = (x - hi).astype(BF16).astype(F32)
    return hi, mid, x - hi - mid


def summed(parts):
    while len(parts) > 1:
        pairs = [a + b for a, b in zip(parts[::2], parts[1::2])]
        parts = pairs + parts[len(pairs) * 2 :]
    return parts[0]


def wrapped(index, size):
    return jnp.where(index >= size, index - size, index)


def kernel(
    n_dp,
    n_tensor,
    scale,
    rows_hbm,
    ids_hbm,
    logits_hbm,
    input_hbm,
    grad_hbm,
    slot_out,
    logit_out,
    router_out,
    ids_ref,
    logits_ref,
    rows,
    inputs,
    grads,
    send,
    recv,
    rows32,
    slot32,
    mine_last,
    other_last,
    score_send,
    score_recv,
    term_send,
    term_recv,
    turned,
    part_send,
    part_recv,
    load_sem,
    send_sem,
    recv_sem,
    ssend_sem,
    srecv_sem,
    tsend_sem,
    trecv_sem,
    psend_sem,
    precv_sem,
    lsend_sem,
    lrecv_sem,
    fsend_sem,
    frecv_sem,
):
    me = lax.axis_index("tensor")
    group = lax.axis_index("dp")
    members = n_tensor // EXPERTS
    capacity = rows.shape[0] // n_tensor
    full = capacity - 1
    segments = rows.shape[1] // LANES
    body = full * segments
    tokens = grads.shape[0]

    barrier = pltpu.get_barrier_semaphore()

    def tensor_peer(i):
        return wrapped(me + i, n_tensor)

    def dp_peer(i):
        return wrapped(group + i, n_dp)

    column, row, core = me // 8, lax.rem(me // 2, 4), lax.rem(me, 2)

    def partner(i, sign):
        part, place = i // 8, i - 8
        middle = (part == 1) | (part == 2)
        along_y = jnp.where(middle, 1 + 2 * lax.rem(i, 2), jnp.where(part == 0, 2, 0))
        rest = jnp.where(middle, place // 2, lax.rem(i, 8))
        along_x = lax.rem(rest // 2 + 1, 4)
        return (
            lax.rem(column + sign * along_x + 4, 4) * 8
            + lax.rem(row + sign * along_y + 4, 4) * 2
            + lax.rem(core + rest + 1, 2)
        )

    load_ids = pltpu.make_async_copy(ids_hbm, ids_ref, load_sem.at[3])
    load_logits = pltpu.make_async_copy(logits_hbm, logits_ref, load_sem.at[4])
    load_grads = pltpu.make_async_copy(grad_hbm, grads, load_sem.at[0])
    load_rows = pltpu.make_async_copy(rows_hbm, rows, load_sem.at[1])
    load_inputs = pltpu.make_async_copy(input_hbm, inputs, load_sem.at[2])
    load_ids.start()
    load_logits.start()
    load_grads.start()

    for i in range(n_tensor - 1):
        pl.semaphore_signal(
            barrier, inc=1, device_id={"tensor": partner(i, 1)}, device_id_type=MESH
        )

    ring = n_dp // 2
    for i in sorted(range(1, n_dp), key=lambda i: -min(i % ring, ring - i % ring)):
        pl.semaphore_signal(barrier, inc=1, device_id={"dp": dp_peer(i)}, device_id_type=MESH)

    load_rows.start()
    load_inputs.start()
    load_ids.wait()
    load_logits.wait()

    id0, id1 = ids_ref[0:1, :], ids_ref[1:2, :]
    logit0, logit1 = logits_ref[0:1, :], logits_ref[1:2, :]
    prob0 = 1.0 / (1.0 + jnp.exp(logit1 - logit0))
    prob1 = 1.0 / (1.0 + jnp.exp(logit0 - logit1))
    experts = iota((EXPERTS, tokens), 0)
    hot0 = jnp.where(experts == id0, 1.0, 0.0)
    hot1 = jnp.where(experts == id1, 1.0, 0.0)
    earlier = jnp.where(
        iota((tokens, tokens), 0) < iota((tokens, tokens), 1), 1.0, 0.0
    ).astype(BF16)
    before = jnp.dot((hot0 + hot1).astype(BF16), earlier, preferred_element_type=F32)
    rank0 = jnp.sum(hot0 * before, axis=0, keepdims=True).astype(jnp.int32)
    rank1 = jnp.sum(hot1 * before, axis=0, keepdims=True).astype(jnp.int32)
    slots = iota((LANES, tokens), 0)
    tail_row = iota((16, LANES), 0)
    prob_row = 2 * segments

    load_grads.wait()
    pl.semaphore_wait(barrier, n_tensor - 1 + n_dp - 1)

    sibling = me + 1 - 2 * core
    tails = pl.ds(0, n_tensor // 2)
    main = pl.ds(0, body)
    last_tile = pl.ds(body, 16)

    def remote(source, target, sent, received, peer):
        return pltpu.make_async_remote_copy(
            src_ref=source,
            dst_ref=target,
            send_sem=sent,
            recv_sem=received,
            device_id={"tensor": peer},
            device_id_type=MESH,
        )

    def for_block(peer, act):
        @pl.when(lax.rem(peer, 2) == core)
        def _():
            act(remote(send.at[peer], recv.at[me], send_sem.at[peer], recv_sem.at[me], peer))

        @pl.when(lax.rem(peer, 2) != core)
        def _():
            act(
                remote(
                    send.at[peer, main],
                    recv.at[me, main],
                    send_sem.at[peer],
                    recv_sem.at[me],
                    peer,
                )
            )

    def start_block(peer):
        for_block(peer, lambda copy: copy.start())

    def sent_block(peer):
        for_block(peer, lambda copy: copy.wait_send())


    def pack(expert):
        key0 = jnp.where(id0 == expert, rank0, -1)
        key1 = jnp.where(id1 == expert, rank1, -1)
        placing = jnp.where((slots == key0) | (slots == key1), 1.0, 0.0).astype(BF16)
        prob = jnp.where(id0 == expert, prob0, jnp.where(id1 == expert, prob1, 0.0))
        hi, mid, lo = split3(prob)
        parts = jnp.where(
            tail_row == prob_row,
            hi,
            jnp.where(tail_row == prob_row + 1, mid, jnp.where(tail_row == prob_row + 2, lo, 0.0)),
        ).astype(BF16)
        slot_probs = lax.dot_general(
            parts, placing, (((1,), (1,)), ((), ())), preferred_element_type=F32
        )
        for k in range(members):
            peer = expert * members + k
            packed = jnp.dot(
                placing[: full + 16],
                grads[:, k * segments * LANES : (k + 1) * segments * LANES],
                preferred_element_type=F32,
            )
            if k % 2 == 0:
                tail = slot_probs
            for j in range(segments):
                piece = packed[:, j * LANES : (j + 1) * LANES]
                send[peer, j * full : (j + 1) * full, :] = piece[:full].astype(BF16)
                place = k % 2 * segments + j
                tail = jnp.where(tail_row == place, piece[full : full + 1], tail)
            if k % 2 == 1:
                send[peer - 1 + core, body : body + 16, :] = tail.astype(BF16)

    half = row // 2

    @pl.loop(0, 4)
    def _(i):
        pack(lax.rem(column + i + 1, 4) * 2 + 1 - half)
        start_block(partner(2 * i, 1))
        start_block(partner(2 * i + 1, 1))

    @pl.loop(0, 4)
    def _(i):
        pack(lax.rem(column + i + 1, 4) * 2 + half)

    @pl.loop(24, n_tensor - 1)
    def _(i):
        start_block(partner(i, 1))

    pltpu.make_async_copy(send.at[me], recv.at[me], recv_sem.at[me]).start()

    @pl.loop(8, 24)
    def _(i):
        start_block(partner(i, 1))

    load_rows.wait()

    @pl.loop(0, rows.shape[0] // 32)
    def _(i):
        at = pl.multiple_of(i * 32, 32)
        for j in range(segments):
            rows32[j, pl.ds(at, 32), :] = rows[
                pl.ds(at, 32), j * LANES : (j + 1) * LANES
            ].astype(F32)

    line_row = iota((8, LANES), 0)

    @pl.loop(0, n_tensor)
    def _(i):
        tile = jnp.zeros((8, LANES), F32)
        for j in range(segments):
            tile = jnp.where(line_row == j, rows32[j, pl.ds(i * capacity + full, 1), :], tile)
        mine_last[i] = tile

    exchange = remote(mine_last, other_last, lsend_sem, lrecv_sem, sibling)
    exchange.start()

    diagonal = iota((full, LANES), 0) == iota((full, LANES), 1)
    lane = iota((1, LANES), 1)

    def remote_scores(index, peer):
        return pltpu.make_async_remote_copy(
            src_ref=score_send.at[peer],
            dst_ref=score_recv.at[index],
            send_sem=ssend_sem,
            recv_sem=srecv_sem,
            device_id={"tensor": peer},
            device_id_type=MESH,
        )

    exchange.wait_recv()

    @pl.loop(0, n_tensor)
    def _(i):
        source = partner(lax.rem(i + 24, n_tensor), -1)
        same = lax.rem(source, 2) == core

        @pl.when(same)
        def _():
            pltpu.make_async_copy(send.at[source], recv.at[source], recv_sem.at[source]).wait()

        @pl.when(lax.rem(source, 2) != core)
        def _():
            pltpu.make_async_copy(
                send.at[source, main], recv.at[source, main], recv_sem.at[source]
            ).wait()

        at = source * capacity
        products = jnp.zeros((full, LANES), F32)
        for j in range(segments):
            piece = recv[source, j * full : (j + 1) * full, :].astype(F32)
            products += piece * rows32[j, pl.ds(at, full), :]
        sums = jnp.sum(products, axis=1, keepdims=True)
        line = jnp.sum(jnp.where(diagonal, sums, 0.0), axis=0, keepdims=True)
        score_send[source] = line

        @pl.when(same)
        def _():
            remote(
                recv.at[source, last_tile],
                recv.at[source, last_tile],
                fsend_sem,
                frecv_sem,
                sibling,
            ).start()
            tail = recv[source, body : body + 16, :].astype(F32)
            mine, other = mine_last[source], other_last[source]
            first = jnp.where(core == 0, mine, other)
            second = jnp.where(core == 0, other, mine)
            last = tail[:8] * first + tail[segments : segments + 8] * second
            last_sum = jnp.sum(jnp.sum(last, axis=0, keepdims=True), axis=1, keepdims=True)
            score_send[source] = jnp.where(lane == full, last_sum, line)

        @pl.when(source != me)
        def _():
            remote_scores(me, source).start()

        @pl.when(source == me)
        def _():
            pltpu.make_async_copy(
                score_send.at[me], score_recv.at[me], srecv_sem
            ).start()

    ranks = iota((LANES, tokens), 0)
    chosen0 = jnp.where(ranks == rank0, 1.0, 0.0).astype(BF16)
    chosen1 = jnp.where(ranks == rank1, 1.0, 0.0).astype(BF16)
    load_inputs.wait()

    pltpu.make_async_copy(score_send, score_recv, srecv_sem).wait()
    scores = jnp.zeros((EXPERTS, LANES), F32)
    for expert in range(EXPERTS):
        total = score_recv[expert * members]
        for k in range(1, members):
            total += score_recv[expert * members + k]
        scores = jnp.where(iota((EXPERTS, LANES), 0) == expert, total, scores)
    hi, mid, lo = split3(scores)
    terms = jnp.concatenate([hi, mid, lo, jnp.zeros_like(lo)], axis=0).astype(BF16)

    def looked_up(chosen, hot):
        found = jnp.dot(terms, chosen, preferred_element_type=F32)
        found = found[:EXPERTS] + found[EXPERTS : 2 * EXPERTS] + found[2 * EXPERTS : 3 * EXPERTS]
        return jnp.sum(found * hot, axis=0, keepdims=True)

    score0 = looked_up(chosen0, hot0)
    score1 = looked_up(chosen1, hot1)
    average = prob0 * score0 + prob1 * score1
    slope0 = prob0 * (score0 - average)
    slope1 = prob1 * (score1 - average)
    logit_out[0:1, :] = slope0
    logit_out[1:2, :] = slope1
    combined = (hot0 * slope0 + hot1 * slope1).astype(BF16)

    def remote_term(index, peer):
        return pltpu.make_async_remote_copy(
            src_ref=term_send.at[peer],
            dst_ref=term_recv.at[index],
            send_sem=tsend_sem,
            recv_sem=trecv_sem,
            device_id={"dp": peer},
            device_id_type=MESH,
        )

    def remote_term(index, peer):
        return pltpu.make_async_remote_copy(
            src_ref=term_send.at[peer],
            dst_ref=term_recv.at[index],
            send_sem=tsend_sem,
            recv_sem=trecv_sem,
            device_id={"dp": peer},
            device_id_type=MESH,
        )

    span = segments * LANES
    quarter = group // segments
    beside = quarter + 1 - 2 * lax.rem(quarter, 2)
    for part in (
        3 - quarter,
        beside,
        lax.rem(quarter + 2, 4),
        quarter,
    ):
        term = jnp.dot(
            combined,
            inputs[:, pl.ds(pl.multiple_of(part * span, span), span)],
            preferred_element_type=F32,
        )
        for j in range(segments):
            term_send[part * segments + j] = term[:, j * LANES : (j + 1) * LANES]
        for j in range(segments):
            peer = part * segments + j

            @pl.when(group != peer)
            def _(peer=peer):
                remote_term(group, peer).start()

    own_term = pltpu.make_async_copy(
        term_send.at[group], term_recv.at[group], trecv_sem
    )
    own_term.start()

    pltpu.make_async_copy(send.at[tails, last_tile], recv.at[tails, last_tile], frecv_sem).wait()

    @pl.loop(0, n_tensor)
    def _(i):
        at = i * capacity
        tail = recv[i, body : body + 16, :].astype(F32)
        prob = (
            tail[prob_row : prob_row + 1]
            + tail[prob_row + 1 : prob_row + 2]
            + tail[prob_row + 2 : prob_row + 3]
        )
        prob_column = jnp.sum(jnp.where(diagonal, prob, 0.0), axis=1, keepdims=True)
        prob_last = jnp.sum(jnp.where(lane == full, prob, 0.0), axis=1, keepdims=True)
        lasts = jnp.where(core == 0, tail[:8], tail[segments : segments + 8]) * prob_last
        for j in range(segments):
            piece = recv[i, j * full : (j + 1) * full, :].astype(F32)
            slot32[j, pl.ds(at, full), :] = piece * prob_column
            slot32[j, pl.ds(at + full, 1), :] = lasts[j : j + 1]

    @pl.loop(0, rows.shape[0] // 32)
    def _(i):
        at = pl.multiple_of(i * 32, 32)
        for j in range(segments):
            slot_out[pl.ds(at, 32), j * LANES : (j + 1) * LANES] = slot32[
                j, pl.ds(at, 32), :
            ].astype(BF16)

    pltpu.make_async_copy(term_send, term_recv, trecv_sem).wait()
    total = summed([term_recv[g] for g in range(n_dp)])

    square = jnp.concatenate([total, jnp.zeros((LANES - EXPERTS, LANES), F32)], axis=0)
    turned[...] = jnp.transpose(square)
    owned = LANES // n_tensor
    lines = turned[pl.ds(0, n_tensor, stride=owned), :]
    for j in range(1, owned):
        lines += pltpu.roll(turned[pl.ds(j, n_tensor, stride=owned), :], j * EXPERTS, 1)
    for i in range(n_tensor):
        part_send[i] = lines[i : i + 1]

    def remote_part(index, peer):
        return pltpu.make_async_remote_copy(
            src_ref=part_send.at[peer],
            dst_ref=part_recv.at[index],
            send_sem=psend_sem,
            recv_sem=precv_sem,
            device_id={"tensor": peer},
            device_id_type=MESH,
        )

    @pl.loop(1, n_tensor, unroll=True)
    def _(i):
        remote_part(me, tensor_peer(i)).start()

    own_part = pltpu.make_async_copy(part_send.at[me], part_recv.at[me], precv_sem)
    own_part.start()

    @pl.loop(1, n_tensor)
    def _(i):
        sent_block(tensor_peer(i))

    remote(mine_last, other_last, lsend_sem, lrecv_sem, sibling).wait_send()
    pltpu.make_async_copy(
        send.at[tails, last_tile], recv.at[tails, last_tile], fsend_sem
    ).wait()

    others = pl.ds(0, n_tensor - 1)
    pltpu.make_async_copy(score_send.at[others], score_recv.at[others], ssend_sem).wait()
    others_dp = pl.ds(0, n_dp - 1)
    pltpu.make_async_copy(term_send.at[others_dp], term_recv.at[others_dp], tsend_sem).wait()

    pltpu.make_async_copy(part_send, part_recv, precv_sem).wait()
    line = summed([part_recv[i] for i in range(n_tensor)]) * scale
    for j in range(owned):
        router_out[j : j + 1, :] = line[:, j * EXPERTS : (j + 1) * EXPERTS]

    pltpu.make_async_copy(part_send.at[others], part_recv.at[others], psend_sem).wait()


def hand_over(chunks, slots, logits, router, slots_out, logits_out, router_out, sem):
    rows = slots.shape[0] // chunks
    parts = [pl.ds(i * rows, rows) for i in range(chunks)]
    copies = [
        pltpu.make_async_copy(slots.at[part], slots_out.at[part], sem.at[i])
        for i, part in enumerate(parts)
    ]
    copies.append(pltpu.make_async_copy(logits, logits_out, sem.at[chunks]))
    copies.append(pltpu.make_async_copy(router, router_out, sem.at[chunks + 1]))
    for copy in copies:
        copy.start()
    for copy in copies:
        copy.wait()


def on_device(expert_rows, expert_ids, gate_logits, layer_input, out_grad):
    n_tensor = lax.axis_size("tensor")
    n_dp = lax.axis_size("dp")
    slot_count, span = expert_rows.shape[2:]
    tokens, width = out_grad.shape
    capacity = slot_count // n_tensor
    segments = span // LANES
    block = (capacity - 1) * segments + 16
    owned = width // (n_dp * n_tensor)
    padded = slot_count + 8
    any_space = pl.BlockSpec(memory_space=pl.ANY)
    in_vmem = pl.BlockSpec(memory_space=pltpu.VMEM)
    dma = pltpu.SemaphoreType.DMA
    slot_grad, logit_grad, router_grad = pl.pallas_call(
        functools.partial(kernel, n_dp, n_tensor, (tokens * n_dp * n_tensor) ** -0.5),
        out_shape=(
            pltpu.VMEM((slot_count, span), BF16),
            pltpu.VMEM((2, tokens), F32),
            pltpu.VMEM((owned, EXPERTS), F32),
        ),
        in_specs=[any_space] * 5,
        out_specs=(in_vmem, in_vmem, in_vmem),
        scratch_shapes=[
            pltpu.VMEM((2, tokens), jnp.int32),
            pltpu.VMEM((2, tokens), F32),
            pltpu.VMEM((slot_count, span), BF16),
            pltpu.VMEM((tokens, width), BF16),
            pltpu.VMEM((tokens, width), BF16),
            pltpu.VMEM((n_tensor, block, LANES), BF16),
            pltpu.VMEM((n_tensor, block, LANES), BF16),
            pltpu.VMEM((segments, padded, LANES), F32),
            pltpu.VMEM((segments, padded, LANES), F32),
            pltpu.VMEM((n_tensor, 8, LANES), F32),
            pltpu.VMEM((n_tensor, 8, LANES), F32),
            pltpu.VMEM((n_tensor, 1, LANES), F32),
            pltpu.VMEM((n_tensor, 1, LANES), F32),
            pltpu.VMEM((n_dp, EXPERTS, LANES), F32),
            pltpu.VMEM((n_dp, EXPERTS, LANES), F32),
            pltpu.VMEM((LANES, LANES), F32),
            pltpu.VMEM((n_tensor, 1, LANES), F32),
            pltpu.VMEM((n_tensor, 1, LANES), F32),
            dma((5,)),
            dma((n_tensor,)),
            dma((n_tensor,)),
            dma,
            dma,
            dma,
            dma,
            dma,
            dma,
            dma,
            dma,
            dma,
            dma,
        ],
        compiler_params=pltpu.CompilerParams(
            collective_id=0, has_side_effects=True, vmem_limit_bytes=56 * 2**20
        ),
    )(
        expert_rows.reshape(slot_count, span),
        expert_ids.T,
        gate_logits.T,
        layer_input,
        out_grad,
    )
    chunks = 6
    slot_grad, logit_grad, router_grad = pl.pallas_call(
        functools.partial(hand_over, chunks),
        out_shape=(
            jax.ShapeDtypeStruct((slot_count, span), BF16),
            jax.ShapeDtypeStruct((2, tokens), F32),
            jax.ShapeDtypeStruct((owned, EXPERTS), F32),
        ),
        in_specs=[any_space] * 3,
        out_specs=(any_space,) * 3,
        scratch_shapes=[dma((chunks + 2,))],
        compiler_params=pltpu.CompilerParams(vmem_limit_bytes=2**20),
    )(slot_grad, logit_grad, router_grad)
    return slot_grad.reshape(expert_rows.shape), logit_grad.T, router_grad


def solution(mesh):
    in_specs = (
        P("dp", "tensor", None, None),
        P(("dp", "tensor"), None),
        P(("dp", "tensor"), None),
        P(("dp", "tensor"), None),
        P(("dp", "tensor"), None),
    )
    out_specs = (
        P("dp", "tensor", None, None),
        P(("dp", "tensor"), None),
        P(("dp", "tensor"), None),
    )
    return jax.shard_map(
        on_device, mesh=mesh, in_specs=in_specs, out_specs=out_specs, check_vma=False
    )
```
